256 devices in a mesh: inst: 16 (over y_lo, z), samp: 16 (over y_hi, x, core).
Axes of the slice: x: 4, y: 4 (y_hi: 2, y_lo: 2; y = y_hi * 2 + y_lo), z: 8, core: 2. Of those that a mesh axis runs over, the one named last changes fastest.
Arguments:
- prompt_key_values: bfloat16 [16, 4096, 2, 1024], P('inst', 'samp'), may hold values from -6 to 6
- match: int32 [16], replicated, may hold values from 0 to 15, each once
- page_list: int32 [16, 16, 16], P('inst'), may hold values from 0 to 255, as said below
- queries: bfloat16 [16, 128, 12288], P('inst', 'samp'), may hold values from -240 to 240
- sample_key_values: bfloat16 [16, 128, 128, 2, 1024], P('inst', 'samp'), may hold values from -10 to 10
- gen_len: int32 [16, 128], P('inst', 'samp'), may hold values from 1 to 128, 8192 in all within a row
Outputs:
- attended: bfloat16 [16, 128, 12288], P('inst', 'samp')
- prompt_pool: bfloat16 [16, 256, 16, 2, 1024], P('inst', 'samp')
The draws below stay inside these ranges and needn't reach their ends.
Inputs may be any that keep to these rules, and one draw needn't show every extreme that they name: `match`: each decode instance continues a different prefill instance. `page_list`: each list holds 16 distinct pages and the lists of one instance together hold every page of the prompt once; of the pages p with p // 16 equal to one value, one owner's list holds at most 2, and exactly 2 for some owner.
All inputs are finite; a program needn't handle non-finite values. No bound on the sum of `gen_len` on one device may be relied on, other than what follows from the above.
Results may differ from the reference program's by a relative error of at most 0.0065.
Values may be sent and summed in bfloat16 or wider, within the bound.
No kernel may reach another device: no remote copies, remote signals or barrier semaphores. Data moves between devices by JAX's collectives and lax.ppermute only.
A program may use at most 128 MiB of HBM per device.

```python
import math
import jax
import jax.numpy as jnp
import numpy as np
from jax import lax

QUERY_HEADS = 96
KEY_VALUE_HEADS = 8
HEAD_FEATURES = 128
PAGE_TOKENS = 16
CAP = 2
GENERATED_LENGTH = 128
PAGES_DEV = 16
PROMPT_PAGES = 256
PROMPT_TOKENS = 4096
DECODE_SAMPLES = 128
N_INST = 16
N_SAMP = 16


def shared_draws(key):
    base_offset = jnp.clip(1.5 * jax.random.normal(jax.random.fold_in(key, 11), (N_INST, DECODE_SAMPLES, GENERATED_LENGTH, 2, KEY_VALUE_HEADS * HEAD_FEATURES), jnp.float32), -9.0, 9.0)
    return base_offset


def draw_sample_key_values(key, part):
    base_offset = shared_draws(key)
    return base_offset.astype(jnp.bfloat16)


def draw_queries(key, part):
    key = jax.random.fold_in(key, 5)
    drawn_result = jnp.clip(2.0 * jax.random.normal(key, (N_INST, DECODE_SAMPLES, QUERY_HEADS * HEAD_FEATURES), jnp.float32), -12.0, 12.0)
    return drawn_result.astype(jnp.bfloat16)


def shuffle_pages(one_key):
    return jax.random.permutation(one_key, PAGES_DEV)


def lists_of_instance(inst_key):
    rounds = PAGES_DEV // CAP
    offsets = jax.random.permutation(jax.random.fold_in(inst_key, 1), N_SAMP)[:rounds]
    slot_table = jax.vmap(shuffle_pages)(jax.random.split(jax.random.fold_in(inst_key, 2), N_SAMP))
    owner = jnp.arange(N_SAMP)[:, None, None]
    turn = jnp.arange(rounds)[None, :, None]
    within = jnp.arange(CAP)[None, None, :]
    sender = (owner - offsets[None, :, None]) % N_SAMP
    sender = jnp.broadcast_to(sender, (N_SAMP, rounds, CAP))
    column = jnp.broadcast_to(turn * CAP + within, (N_SAMP, rounds, CAP))
    slot = slot_table[sender, column]
    pages = (sender * PAGES_DEV + slot).reshape(N_SAMP, PAGES_DEV)
    orders = jax.vmap(shuffle_pages)(jax.random.split(jax.random.fold_in(inst_key, 3), N_SAMP))
    return jnp.take_along_axis(pages, orders, axis=1).astype(jnp.int32)


def draw_page_list(key, part):
    key = jax.random.fold_in(key, 7)
    return jax.vmap(lists_of_instance)(jax.random.split(key, N_INST))


def steps_of(rng, dims, cuts, smallest, top_value):
    gain, own = 1.0, jax.random.fold_in(rng, 6)
    for axis_at, blocks in cuts:
        heights = jnp.exp(jax.random.uniform(jax.random.fold_in(own, axis_at), (blocks,), jnp.float32, smallest / len(cuts), top_value / len(cuts)))
        gain = gain * jnp.repeat(heights, dims[axis_at] // blocks).reshape([-1 if axis == axis_at else 1 for axis in range(len(dims))])
    return gain


def length_profile(number_of, total, bound, lean):
    weights = [(1 << 20) // math.isqrt(standing ** lean) + 1 for standing in range(2, number_of + 1)]
    surplus, counts = total - bound - (number_of - 1), [1] * (number_of - 1)
    while surplus > 0:
        movable = [i for i in range(number_of - 1) if counts[i] < bound]
        pool, remaining = sum([weights[i] for i in movable]), surplus
        for i in movable:
            more = min(bound - counts[i], max(1, remaining * weights[i] // pool), surplus)
            counts[i] = counts[i] + more
            surplus = surplus - more
    return np.array([bound] + counts)


def ragged_sizes(own_key, amount, total, limit, skew):
    if amount == 2:
        one = jax.random.randint(own_key, (), max(1, total - limit), min(limit, total - 1) + 1)
        return jnp.stack([one, total - one])
    sizes = jnp.asarray(length_profile(amount, total, limit, skew), jnp.int32)
    couples = (amount - 1) // 2
    donor, receiver = sizes[1:1 + 2 * couples:2], sizes[2:2 + 2 * couples:2]
    slack = jnp.minimum(donor - 1, limit - receiver)
    passed = jax.random.randint(jax.random.fold_in(own_key, 1), (couples,), 0, 1 << 20) % (slack + 1)
    sizes = sizes.at[1:1 + 2 * couples:2].set(donor - passed).at[2:2 + 2 * couples:2].set(receiver + passed)
    return sizes[jax.random.permutation(jax.random.fold_in(own_key, 2), amount)]


def noise(key, dims, scale, bound, cuts=(), kind=jnp.bfloat16):
    loudness = steps_of(key, dims, cuts, -0.22, 0.18) if cuts else 1.0
    entries = jax.random.normal(key, dims, jnp.float32) * scale * loudness
    return jnp.minimum(jnp.maximum(entries, -bound), bound).astype(kind)


def setup_inputs(seed: int = 0) -> dict:
    arg_keys = jax.random.split(jax.random.key(seed), 7)
    prompt_key_values = noise(arg_keys[0], (N_INST, PROMPT_TOKENS, 2, KEY_VALUE_HEADS * HEAD_FEATURES), 1.0, 6.0, ((0, 16), (1, 16)))
    match = jax.random.permutation(arg_keys[1], N_INST).astype(jnp.int32)
    page_list = draw_page_list(jax.random.fold_in(arg_keys[6], 71), 0)
    queries = draw_queries(jax.random.fold_in(arg_keys[6], 71), 0)
    sample_key_values = draw_sample_key_values(jax.random.fold_in(arg_keys[6], 71), 0)
    gen_len = jax.vmap(lambda own: ragged_sizes(own, DECODE_SAMPLES, DECODE_SAMPLES * GENERATED_LENGTH // 2, GENERATED_LENGTH, 2))(jax.random.split(arg_keys[5], N_INST)).reshape((N_INST, DECODE_SAMPLES)).astype(jnp.int32)
    return {"prompt_key_values": prompt_key_values, "match": match, "page_list": page_list, "queries": queries, "sample_key_values": sample_key_values, "gen_len": gen_len}


def reference(prompt_key_values, match, page_list, queries, sample_key_values, gen_len):
    group_count = QUERY_HEADS // KEY_VALUE_HEADS
    scale = HEAD_FEATURES ** -0.5

    def one_instance(inputs):
        source, list_table, query_matrix, sample_cache, lengths = inputs
        prompt_index = jnp.take(prompt_key_values, source, axis=0)
        page_token_rows = prompt_index.reshape(PROMPT_PAGES, PAGE_TOKENS, 2, KEY_VALUE_HEADS * HEAD_FEATURES)
        page_pool = jnp.take(page_token_rows, list_table.reshape(-1), axis=0)
        query_head_rows = query_matrix.astype(jnp.float32).reshape(DECODE_SAMPLES, KEY_VALUE_HEADS, group_count, HEAD_FEATURES)
        prefix_keys = prompt_index[:, 0, :].astype(jnp.float32).reshape(PROMPT_TOKENS, KEY_VALUE_HEADS, HEAD_FEATURES)
        prefix_values = prompt_index[:, 1, :].astype(jnp.float32).reshape(PROMPT_TOKENS, KEY_VALUE_HEADS, HEAD_FEATURES)
        sample_keys = sample_cache[:, :, 0, :].astype(jnp.float32).reshape(DECODE_SAMPLES, GENERATED_LENGTH, KEY_VALUE_HEADS, HEAD_FEATURES)
        sample_values = sample_cache[:, :, 1, :].astype(jnp.float32).reshape(DECODE_SAMPLES, GENERATED_LENGTH, KEY_VALUE_HEADS, HEAD_FEATURES)
        prompt_scores = jnp.einsum("shgd,nhd->shgn", query_head_rows, prefix_keys) * scale
        own_scores = jnp.einsum("shgd,snhd->shgn", query_head_rows, sample_keys) * scale
        live_mask = jnp.arange(GENERATED_LENGTH, dtype=jnp.int32)[None, :] < lengths[:, None]
        own_scores = jnp.where(live_mask[:, None, None, :], own_scores, -jnp.inf)
        peak = jnp.maximum(jnp.max(prompt_scores, axis=-1), jnp.max(own_scores, axis=-1))
        prompt_weights = jnp.exp(prompt_scores - peak[..., None])
        own_weights = jnp.exp(own_scores - peak[..., None])
        weight_sum = jnp.sum(prompt_weights, axis=-1) + jnp.sum(own_weights, axis=-1)
        prompt_rounded = prompt_weights.astype(jnp.bfloat16).astype(jnp.float32)
        own_rounded = own_weights.astype(jnp.bfloat16).astype(jnp.float32)
        numerator = jnp.einsum("shgn,nhd->shgd", prompt_rounded, prefix_values)
        numerator = numerator + jnp.einsum("shgn,snhd->shgd", own_rounded, sample_values)
        attended = (numerator / weight_sum[..., None]).astype(jnp.bfloat16)
        return attended.reshape(DECODE_SAMPLES, QUERY_HEADS * HEAD_FEATURES), page_pool

    attended, pools = lax.map(one_instance, (match, page_list, queries, sample_key_values, gen_len))
    return attended, pools
```

```python
import functools
import math

import jax
import jax.numpy as jnp
from jax import lax
from jax.experimental import pallas as pl
from jax.experimental.pallas import tpu as pltpu
from jax.sharding import PartitionSpec as P

QUERY_HEADS = 96
KEY_VALUE_HEADS = 8
HEAD_FEATURES = 128
PAGE_TOKENS = 16
GROUP = QUERY_HEADS // KEY_VALUE_HEADS
WIDTH = GROUP * HEAD_FEATURES
SCALE = HEAD_FEATURES ** (-0.5)


def partial_own(query_rows, sample_keys, sample_values, live_mask):
    count = query_rows.shape[0]
    peaks = []
    sums = []
    numers = []
    for head in range(KEY_VALUE_HEADS):
        block = query_rows[:, head * WIDTH : (head + 1) * WIDTH].reshape(
            count, GROUP, HEAD_FEATURES
        )
        key_block = sample_keys[:, :, head * HEAD_FEATURES : (head + 1) * HEAD_FEATURES]
        value_block = sample_values[:, :, head * HEAD_FEATURES : (head + 1) * HEAD_FEATURES]
        scores = jnp.einsum(
            "sgd,snd->sgn", block, key_block, preferred_element_type=jnp.float32
        ) * SCALE
        scores = jnp.where(live_mask[:, None, :], scores, -jnp.inf)
        peak = jnp.max(scores, axis=-1)
        weights = jnp.exp(scores - peak[..., None])
        weight_sum = jnp.sum(weights, axis=-1)
        numer = jnp.einsum(
            "sgn,snd->sgd",
            weights.astype(jnp.bfloat16),
            value_block,
            preferred_element_type=jnp.float32,
        )
        peaks.append(peak)
        sums.append(weight_sum)
        numers.append(numer)
    return (jnp.stack(peaks, axis=1), jnp.stack(sums, axis=1), jnp.stack(numers, axis=1))


def split3(x):
    high = x.astype(jnp.bfloat16)
    rest = x - high.astype(jnp.float32)
    middle = rest.astype(jnp.bfloat16)
    low = (rest - middle.astype(jnp.float32)).astype(jnp.bfloat16)
    return high, middle, low


def shared_kernel(head_ref, query_ref, pair_ref, out_ref, key_ref, value_ref):
    pieces = pair_ref.shape[0]
    samples = query_ref.shape[0]
    row = lax.broadcasted_iota(jnp.int32, (256, 256), 0)
    column = lax.broadcasted_iota(jnp.int32, (256, 256), 1)
    wanted = jnp.where(row < 128, 2 * row, 2 * (row - 128) + 1)
    pick = jnp.where(column == wanted, 1.0, 0.0).astype(jnp.bfloat16)
    for step in range(pieces // 16):
        both = pair_ref[step * 16 : (step + 1) * 16].reshape(256, HEAD_FEATURES)
        apart = jnp.dot(pick, both, preferred_element_type=jnp.float32).astype(jnp.bfloat16)
        key_ref[step * 128 : (step + 1) * 128, :] = apart[:128]
        value_ref[step * 128 : (step + 1) * 128, :] = apart[128:]
    factor = SCALE * math.log2(math.e)
    lane = lax.broadcasted_iota(jnp.int32, (samples, 128), 1)

    def group(g, stats):
        start = pl.multiple_of(g * HEAD_FEATURES, HEAD_FEATURES)
        query = query_ref[:, pl.ds(start, HEAD_FEATURES)]
        scores = lax.dot_general(
            query, key_ref[...], (((1,), (1,)), ((), ())), preferred_element_type=jnp.float32
        )
        top = jnp.max(scores, axis=-1, keepdims=True)
        weights = jnp.exp2((scores - top) * factor)
        total = jnp.sum(weights, axis=-1, keepdims=True)
        numer = jnp.dot(
            weights.astype(jnp.bfloat16), value_ref[...], preferred_element_type=jnp.float32
        )
        out_ref[:, pl.ds(start, HEAD_FEATURES)] = numer.astype(jnp.bfloat16)
        for place, term in enumerate(split3(top * SCALE) + split3(total)):
            stats = jnp.where(
                lane == place * GROUP + g, term.astype(jnp.float32), stats
            )
        return stats

    stats = lax.fori_loop(0, GROUP, group, jnp.zeros((samples, 128), jnp.float32))
    out_ref[:, WIDTH:] = stats.astype(jnp.bfloat16)


def partial_shared(head, query_rows, pairs):
    samples = query_rows.shape[0]
    tokens = pairs.shape[0] * 8
    return pl.pallas_call(
        shared_kernel,
        out_shape=jax.ShapeDtypeStruct((samples, WIDTH + 128), jnp.bfloat16),
        grid_spec=pltpu.PrefetchScalarGridSpec(
            num_scalar_prefetch=1,
            grid=(1,),
            in_specs=[
                pl.BlockSpec((samples, WIDTH), lambda i, head: (0, head[0])),
                pl.BlockSpec(pairs.shape, lambda i, head: (0, 0, 0)),
            ],
            out_specs=pl.BlockSpec((samples, WIDTH + 128), lambda i, head: (0, 0)),
            scratch_shapes=[
                pltpu.VMEM((tokens, HEAD_FEATURES), jnp.bfloat16),
                pltpu.VMEM((tokens, HEAD_FEATURES), jnp.bfloat16),
            ],
        ),
        compiler_params=pltpu.CompilerParams(vmem_limit_bytes=32 * 1024 * 1024),
        cost_estimate=pl.CostEstimate(
            flops=4 * samples * GROUP * tokens * HEAD_FEATURES,
            bytes_accessed=4 * 1024 * 1024,
            transcendentals=samples * GROUP * tokens,
        ),
    )(head, query_rows, pairs)


def body(n_inst, n_samp, prompt_key_values, match, page_list, queries, sample_key_values, gen_len):
    local_total = queries.shape[1]
    pages_dev = page_list.shape[2]
    half = PAGE_TOKENS // 2
    member = lax.axis_index("samp")
    local_queries = queries[0]

    all_queries = lax.all_gather(local_queries, "samp", axis=0, tiled=True)

    pages = lax.all_to_all(prompt_key_values, "inst", split_axis=1, concat_axis=0, tiled=True)

    sample_keys = sample_key_values[0, :, :, 0, :]
    sample_values = sample_key_values[0, :, :, 1, :]
    live_mask = jnp.arange(sample_keys.shape[1], dtype=jnp.int32)[None, :] < gen_len[0][:, None]
    own_peak, own_sum, own_numer = partial_own(local_queries, sample_keys, sample_values, live_mask)

    chosen = jnp.take(pages, match, axis=0)
    chosen = chosen.reshape(n_inst, PAGE_TOKENS, 2, KEY_VALUE_HEADS, HEAD_FEATURES)
    chosen = chosen.transpose(0, 3, 1, 2, 4).reshape(n_inst * n_samp, half * 2, HEAD_FEATURES)
    pairs = lax.all_to_all(chosen, ("inst", "samp"), split_axis=0, concat_axis=0, tiled=True)

    listed = page_list[0].reshape(-1)
    place = (listed % pages_dev) * n_samp + listed // pages_dev
    sent = jnp.take(pairs, place, axis=0)
    came = lax.all_to_all(
        sent.reshape(n_samp, pages_dev, half * 2, HEAD_FEATURES),
        "samp", split_axis=0, concat_axis=0, tiled=True,
    )
    came = came.reshape(KEY_VALUE_HEADS, 2, pages_dev, half, 2, HEAD_FEATURES)
    page_pool = came.transpose(2, 1, 3, 4, 0, 5).reshape(
        1, pages_dev, PAGE_TOKENS, 2, KEY_VALUE_HEADS * HEAD_FEATURES
    )

    part = partial_shared((member // 2).astype(jnp.int32)[None], all_queries, pairs)
    back = lax.all_to_all(
        part.reshape(n_samp, local_total, WIDTH + 128),
        "samp", split_axis=0, concat_axis=0, tiled=True,
    )
    back = back.reshape(KEY_VALUE_HEADS, 2, local_total, WIDTH + 128)
    numer = back[..., :WIDTH].reshape(KEY_VALUE_HEADS, 2, local_total, GROUP, HEAD_FEATURES)
    numer = numer.astype(jnp.float32)
    stats = back[..., WIDTH : WIDTH + 6 * GROUP].astype(jnp.float32)
    stats = stats.reshape(KEY_VALUE_HEADS, 2, local_total, 2, 3, GROUP)
    stats = (stats[..., 0, :] + stats[..., 1, :]) + stats[..., 2, :]
    peaks = stats[..., 0, :]
    sums = stats[..., 1, :]

    own_peak = own_peak.transpose(1, 0, 2)
    own_sum = own_sum.transpose(1, 0, 2)
    own_numer = own_numer.transpose(1, 0, 2, 3)
    peak = jnp.maximum(jnp.max(peaks, axis=1), own_peak)
    scales = jnp.exp(peaks - peak[:, None])
    own_scale = jnp.exp(own_peak - peak)
    weight_sum = jnp.sum(sums * scales, axis=1) + own_sum * own_scale
    total = jnp.sum(numer * scales[..., None], axis=1) + own_numer * own_scale[..., None]
    attended = (total / weight_sum[..., None]).astype(jnp.bfloat16)
    attended = attended.transpose(1, 0, 2, 3).reshape(1, local_total, QUERY_HEADS * HEAD_FEATURES)
    return (attended, page_pool)


def solution(mesh):
    in_specs = (
        P("inst", "samp", None, None),
        P(),
        P("inst", None, None),
        P("inst", "samp", None),
        P("inst", "samp", None, None, None),
        P("inst", "samp"),
    )
    out_specs = (P("inst", "samp", None), P("inst", "samp", None, None, None))
    step = functools.partial(body, mesh.shape["inst"], mesh.shape["samp"])
    return jax.shard_map(step, mesh=mesh, in_specs=in_specs, out_specs=out_specs, check_vma=False)
```

```python
import functools
import math

import jax
import jax.numpy as jnp
from jax import lax
from jax.experimental import pallas as pl
from jax.experimental.pallas import tpu as pltpu
from jax.sharding import PartitionSpec as P

QUERY_HEADS = 96
KEY_VALUE_HEADS = 8
HEAD_FEATURES = 128
PAGE_TOKENS = 16
GROUP = QUERY_HEADS // KEY_VALUE_HEADS
WIDTH = GROUP * HEAD_FEATURES
SCALE = HEAD_FEATURES ** (-0.5)


def partial_own(query_rows, sample_keys, sample_values, live_mask):
    count = query_rows.shape[0]
    peaks = []
    sums = []
    numers = []
    for head in range(KEY_VALUE_HEADS):
        block = query_rows[:, head * WIDTH : (head + 1) * WIDTH].reshape(
            count, GROUP, HEAD_FEATURES
        )
        key_block = sample_keys[:, :, head * HEAD_FEATURES : (head + 1) * HEAD_FEATURES]
        value_block = sample_values[:, :, head * HEAD_FEATURES : (head + 1) * HEAD_FEATURES]
        scores = jnp.einsum(
            "sgd,snd->sgn", block, key_block, preferred_element_type=jnp.float32
        ) * SCALE
        scores = jnp.where(live_mask[:, None, :], scores, -jnp.inf)
        peak = jnp.max(scores, axis=-1)
        weights = jnp.exp(scores - peak[..., None])
        weight_sum = jnp.sum(weights, axis=-1)
        numer = jnp.einsum(
            "sgn,snd->sgd",
            weights.astype(jnp.bfloat16),
            value_block,
            preferred_element_type=jnp.float32,
        )
        peaks.append(peak)
        sums.append(weight_sum)
        numers.append(numer)
    return (jnp.stack(peaks, axis=1), jnp.stack(sums, axis=1), jnp.stack(numers, axis=1))


def split3(x):
    high = x.astype(jnp.bfloat16)
    rest = x - high.astype(jnp.float32)
    middle = rest.astype(jnp.bfloat16)
    low = (rest - middle.astype(jnp.float32)).astype(jnp.bfloat16)
    return high, middle, low


def shared_kernel(place_ref, query_ref, pair_ref, out_ref, key_ref, value_ref):
    pieces = pair_ref.shape[0]
    samples = query_ref.shape[0]
    owners, rows = out_ref.shape[0], pair_ref.shape[1]
    slots = pieces // owners
    local = samples // owners

    def move(n, carry):
        row = pl.multiple_of(lax.rem(n, slots) * rows, rows)
        out_ref[lax.div(n, slots), pl.ds(row, rows), :] = pair_ref[place_ref[n]]
        return carry

    lax.fori_loop(0, pieces, move, 0, unroll=8)

    row = lax.broadcasted_iota(jnp.int32, (256, 256), 0)
    column = lax.broadcasted_iota(jnp.int32, (256, 256), 1)
    wanted = jnp.where(row < 128, 2 * row, 2 * (row - 128) + 1)
    pick = jnp.where(column == wanted, 1.0, 0.0).astype(jnp.bfloat16)
    for step in range(pieces // 16):
        both = pair_ref[step * 16 : (step + 1) * 16].reshape(256, HEAD_FEATURES)
        apart = jnp.dot(pick, both, preferred_element_type=jnp.float32).astype(jnp.bfloat16)
        key_ref[step * 128 : (step + 1) * 128, :] = apart[:128]
        value_ref[step * 128 : (step + 1) * 128, :] = apart[128:]

    factor = SCALE * math.log2(math.e)
    lane = lax.broadcasted_iota(jnp.int32, (samples, 128), 1)
    peaks = jnp.zeros((samples, 128), jnp.float32)
    sums = jnp.zeros((samples, 128), jnp.float32)

    def side_by_side(low, high):
        low = low.reshape(owners, local, HEAD_FEATURES)
        high = high.reshape(owners, local, HEAD_FEATURES)
        return jnp.concatenate([low, high], axis=1).astype(jnp.bfloat16)

    for g in range(0, GROUP, 2):
        query = jnp.concatenate(
            [
                query_ref[:, g * HEAD_FEATURES : (g + 1) * HEAD_FEATURES],
                query_ref[:, (g + 1) * HEAD_FEATURES : (g + 2) * HEAD_FEATURES],
            ],
            axis=0,
        )
        scores = lax.dot_general(
            query, key_ref[...], (((1,), (1,)), ((), ())), preferred_element_type=jnp.float32
        )
        top = jnp.max(scores, axis=-1, keepdims=True)
        weights = jnp.exp2((scores - top) * factor)
        total = jnp.sum(weights, axis=-1, keepdims=True)
        numer = jnp.dot(
            weights.astype(jnp.bfloat16), value_ref[...], preferred_element_type=jnp.float32
        )
        first = slots * rows + g * local
        out_ref[:, first : first + 2 * local, :] = side_by_side(numer[:samples], numer[samples:])
        top = top * SCALE
        peaks = jnp.where(lane == g, top[:samples], peaks)
        peaks = jnp.where(lane == g + 1, top[samples:], peaks)
        sums = jnp.where(lane == g, total[:samples], sums)
        sums = jnp.where(lane == g + 1, total[samples:], sums)

    stats = jnp.zeros((samples, 128), jnp.float32)
    for place, term in enumerate(split3(peaks) + split3(sums)):
        term = term.astype(jnp.float32)
        stats = stats + (pltpu.roll(term, place * GROUP, 1) if place else term)
    first = slots * rows + GROUP * local
    out_ref[:, first:, :] = side_by_side(stats, jnp.zeros_like(stats))


def partial_shared(place, query_rows, pairs, owners):
    samples = query_rows.shape[0]
    pieces, rows, features = pairs.shape
    tokens = pieces * rows // 2
    sent = pieces // owners * rows + (GROUP + 2) * (samples // owners)
    return pl.pallas_call(
        shared_kernel,
        out_shape=jax.ShapeDtypeStruct((owners, sent, features), jnp.bfloat16),
        in_specs=[
            pl.BlockSpec(memory_space=pltpu.SMEM),
            pl.BlockSpec(memory_space=pltpu.VMEM),
            pl.BlockSpec(memory_space=pltpu.VMEM),
        ],
        out_specs=pl.BlockSpec(memory_space=pltpu.VMEM),
        scratch_shapes=[
            pltpu.VMEM((tokens, features), jnp.bfloat16),
            pltpu.VMEM((tokens, features), jnp.bfloat16),
        ],
        compiler_params=pltpu.CompilerParams(vmem_limit_bytes=40 * 1024 * 1024),
        cost_estimate=pl.CostEstimate(
            flops=4 * samples * GROUP * tokens * features,
            bytes_accessed=4 * 1024 * 1024,
            transcendentals=samples * GROUP * tokens,
        ),
    )(place, query_rows, pairs)


def finish_kernel(tile_ref, came_ref, numer_ref, stats_ref, out_ref, pool_ref, sems):
    senders = came_ref.shape[0]
    slots = pool_ref.shape[0]
    local = out_ref.shape[0]
    half = tile_ref.shape[2]
    pool_rows = slots * half * 2
    copies = []
    for sender in range(senders):
        head, part = sender // 2, sender % 2
        copies.append(
            pltpu.make_async_copy(
                tile_ref.at[sender, 0:slots],
                pool_ref.at[
                    :,
                    part * half : (part + 1) * half,
                    :,
                    head * HEAD_FEATURES : (head + 1) * HEAD_FEATURES,
                ],
                sems.at[sender],
            )
        )
        copies[-1].start()

    first = pool_rows + GROUP * local

    def back(x, places):
        return pltpu.roll(x, 128 - places, 1)

    for head in range(KEY_VALUE_HEADS):
        peaks = [stats_ref[head, 0]]
        sums = [stats_ref[head, 1]]
        for part in range(2):
            terms = came_ref[2 * head + part, first : first + 2 * local, :]
            terms = terms.astype(jnp.float32)[:local]
            terms = (terms + back(terms, GROUP)) + back(terms, 2 * GROUP)
            peaks.append(terms)
            sums.append(back(terms, 3 * GROUP))
        peak = jnp.maximum(jnp.maximum(peaks[0], peaks[1]), peaks[2])
        scales = [jnp.exp(p - peak) for p in peaks]
        total = (sums[0] * scales[0] + sums[1] * scales[1]) + sums[2] * scales[2]
        scales = [s / total for s in scales]
        for g in range(0, GROUP, 2):
            rows = slice(g * local, (g + 2) * local)
            numers = [numer_ref[head, rows]] + [
                came_ref[
                    2 * head + part, pool_rows + g * local : pool_rows + (g + 2) * local, :
                ].astype(jnp.float32)
                for part in range(2)
            ]
            for k in range(2):
                mine = [n[k * local : (k + 1) * local] for n in numers]
                by = [s[:, g + k : g + k + 1] for s in scales]
                value = (mine[0] * by[0] + mine[1] * by[1]) + mine[2] * by[2]
                column = (head * GROUP + g + k) * HEAD_FEATURES
                out_ref[:, column : column + HEAD_FEATURES] = value.astype(jnp.bfloat16)

    for copy in copies:
        copy.wait()


def finish(came, numer, stats, local, slots):
    senders, rows, features = came.shape
    half = PAGE_TOKENS // 2
    tiles = came.reshape(senders, rows // (2 * half), half, 2, features)
    return pl.pallas_call(
        finish_kernel,
        out_shape=(
            jax.ShapeDtypeStruct((local, QUERY_HEADS * HEAD_FEATURES), jnp.bfloat16),
            jax.ShapeDtypeStruct(
                (slots, PAGE_TOKENS, 2, KEY_VALUE_HEADS * HEAD_FEATURES), jnp.bfloat16
            ),
        ),
        in_specs=[
            pl.BlockSpec(memory_space=pl.ANY),
            pl.BlockSpec(memory_space=pltpu.VMEM),
            pl.BlockSpec(memory_space=pltpu.VMEM),
            pl.BlockSpec(memory_space=pltpu.VMEM),
        ],
        out_specs=(pl.BlockSpec(memory_space=pltpu.VMEM), pl.BlockSpec(memory_space=pl.ANY)),
        scratch_shapes=[pltpu.SemaphoreType.DMA((senders,))],
        compiler_params=pltpu.CompilerParams(vmem_limit_bytes=32 * 1024 * 1024),
        cost_estimate=pl.CostEstimate(
            flops=6 * local * QUERY_HEADS * HEAD_FEATURES,
            bytes_accessed=4 * 1024 * 1024,
            transcendentals=0,
        ),
    )(tiles, came, numer, stats)


def gather_queries(local_queries, member, n_samp):
    local = local_queries.shape[0]
    held = local_queries.reshape(local, KEY_VALUE_HEADS, WIDTH).transpose(1, 0, 2)
    for step, place in enumerate((3, 2, 1, 0)):
        bit = (member >> place) & 1
        if place:
            half = held.shape[0] // 2
            kept = lax.dynamic_slice_in_dim(held, bit * half, half, 0)
            sent = lax.dynamic_slice_in_dim(held, (1 - bit) * half, half, 0)
        else:
            kept = sent = held
        pairs = [(i, i ^ (1 << place)) for i in range(n_samp)]
        came = lax.ppermute(sent, "samp", pairs)
        held = jnp.stack(
            [jnp.where(bit == 0, kept, came), jnp.where(bit == 0, came, kept)], axis=1 + step
        )
    return held.reshape(n_samp * local, WIDTH)


def body(n_inst, n_samp, prompt_key_values, match, page_list, queries, sample_key_values, gen_len):
    local_total = queries.shape[1]
    pages_dev = page_list.shape[2]
    half = PAGE_TOKENS // 2
    member = lax.axis_index("samp")
    local_queries = queries[0]

    pages = lax.all_to_all(prompt_key_values, "inst", split_axis=1, concat_axis=0, tiled=True)

    head_queries = gather_queries(local_queries, member, n_samp)

    sample_keys = sample_key_values[0, :, :, 0, :]
    sample_values = sample_key_values[0, :, :, 1, :]
    live_mask = jnp.arange(sample_keys.shape[1], dtype=jnp.int32)[None, :] < gen_len[0][:, None]
    own_peak, own_sum, own_numer = partial_own(local_queries, sample_keys, sample_values, live_mask)
    own_stats = jnp.stack([own_peak.transpose(1, 0, 2), own_sum.transpose(1, 0, 2)], axis=1)
    own_stats = jnp.pad(own_stats, ((0, 0), (0, 0), (0, 0), (0, 128 - GROUP)))
    own_numer = own_numer.transpose(1, 2, 0, 3).reshape(
        KEY_VALUE_HEADS, GROUP * local_total, HEAD_FEATURES
    )

    listed = page_list[0].reshape(-1)
    place = (listed % pages_dev) * n_samp + listed // pages_dev

    chosen = pages.at[match].get(mode="promise_in_bounds")
    chosen = chosen.reshape(n_inst, PAGE_TOKENS, 2, KEY_VALUE_HEADS, HEAD_FEATURES)
    chosen = chosen.transpose(0, 3, 1, 2, 4).reshape(n_inst * n_samp, half * 2, HEAD_FEATURES)
    pairs = lax.all_to_all(chosen, ("inst", "samp"), split_axis=0, concat_axis=0, tiled=True)
    pairs, place, head_queries, own_stats, own_numer = lax.optimization_barrier(
        (pairs, place, head_queries, own_stats, own_numer)
    )

    sent = partial_shared(place, head_queries, pairs, n_samp)
    came = lax.all_to_all(sent, "samp", split_axis=0, concat_axis=0, tiled=True)
    attended, page_pool = finish(came, own_numer, own_stats, local_total, pages_dev)
    return (attended[None], page_pool[None])


def solution(mesh):
    in_specs = (
        P("inst", "samp", None, None),
        P(),
        P("inst", None, None),
        P("inst", "samp", None),
        P("inst", "samp", None, None, None),
        P("inst", "samp"),
    )
    out_specs = (P("inst", "samp", None), P("inst", "samp", None, None, None))
    step = functools.partial(body, mesh.shape["inst"], mesh.shape["samp"])
    return jax.shard_map(step, mesh=mesh, in_specs=in_specs, out_specs=out_specs, check_vma=False)
```

```python
import functools
import math

import jax
import jax.numpy as jnp
from jax import lax
from jax.experimental import pallas as pl
from jax.experimental.pallas import tpu as pltpu
from jax.sharding import PartitionSpec as P

QUERY_HEADS = 96
KEY_VALUE_HEADS = 8
HEAD_FEATURES = 128
PAGE_TOKENS = 16
GROUP = QUERY_HEADS // KEY_VALUE_HEADS
WIDTH = GROUP * HEAD_FEATURES
SCALE = HEAD_FEATURES ** (-0.5)


def partial_own(query_rows, sample_keys, sample_values, live_mask):
    count = query_rows.shape[0]
    peaks = []
    sums = []
    numers = []
    for head in range(KEY_VALUE_HEADS):
        block = query_rows[:, head * WIDTH : (head + 1) * WIDTH].reshape(
            count, GROUP, HEAD_FEATURES
        )
        key_block = sample_keys[:, :, head * HEAD_FEATURES : (head + 1) * HEAD_FEATURES]
        value_block = sample_values[:, :, head * HEAD_FEATURES : (head + 1) * HEAD_FEATURES]
        scores = jnp.einsum(
            "sgd,snd->sgn", block, key_block, preferred_element_type=jnp.float32
        ) * SCALE
        scores = jnp.where(live_mask[:, None, :], scores, -jnp.inf)
        peak = jnp.max(scores, axis=-1)
        weights = jnp.exp(scores - peak[..., None])
        weight_sum = jnp.sum(weights, axis=-1)
        numer = jnp.einsum(
            "sgn,snd->sgd",
            weights.astype(jnp.bfloat16),
            value_block,
            preferred_element_type=jnp.float32,
        )
        peaks.append(peak)
        sums.append(weight_sum)
        numers.append(numer)
    return (jnp.stack(peaks, axis=1), jnp.stack(sums, axis=1), jnp.stack(numers, axis=1))


def split3(x):
    high = x.astype(jnp.bfloat16)
    rest = x - high.astype(jnp.float32)
    middle = rest.astype(jnp.bfloat16)
    low = (rest - middle.astype(jnp.float32)).astype(jnp.bfloat16)
    return high, middle, low


def shared_kernel(place_ref, query_ref, pair_ref, out_ref, key_ref, value_ref):
    pieces = pair_ref.shape[0]
    samples = query_ref.shape[0]
    owners, rows = out_ref.shape[0], pair_ref.shape[1]
    slots = pieces // owners
    local = samples // owners

    row = lax.broadcasted_iota(jnp.int32, (256, 256), 0)
    column = lax.broadcasted_iota(jnp.int32, (256, 256), 1)
    wanted = jnp.where(row < 128, 2 * row, 2 * (row - 128) + 1)
    pick = jnp.where(column == wanted, 1.0, 0.0).astype(jnp.bfloat16)
    for step in range(pieces // 16):
        both = pair_ref[step * 16 : (step + 1) * 16].reshape(256, HEAD_FEATURES)
        apart = jnp.dot(pick, both, preferred_element_type=jnp.float32).astype(jnp.bfloat16)
        key_ref[step * 128 : (step + 1) * 128, :] = apart[:128]
        value_ref[step * 128 : (step + 1) * 128, :] = apart[128:]
        for n in range(step * 16, (step + 1) * 16):
            row = n % slots * rows
            out_ref[n // slots, row : row + rows, :] = pair_ref[place_ref[n]]

    factor = SCALE * math.log2(math.e)
    lane = lax.broadcasted_iota(jnp.int32, (samples, 128), 1)
    peaks = jnp.zeros((samples, 128), jnp.float32)
    sums = jnp.zeros((samples, 128), jnp.float32)

    def side_by_side(low, high):
        low = low.reshape(owners, local, HEAD_FEATURES)
        high = high.reshape(owners, local, HEAD_FEATURES)
        return jnp.concatenate([low, high], axis=1).astype(jnp.bfloat16)

    for g in range(0, GROUP, 2):
        query = jnp.concatenate(
            [
                query_ref[:, g * HEAD_FEATURES : (g + 1) * HEAD_FEATURES],
                query_ref[:, (g + 1) * HEAD_FEATURES : (g + 2) * HEAD_FEATURES],
            ],
            axis=0,
        )
        scores = lax.dot_general(
            query, key_ref[...], (((1,), (1,)), ((), ())), preferred_element_type=jnp.float32
        )
        top = jnp.max(scores, axis=-1, keepdims=True)
        weights = jnp.exp2((scores - top) * factor)
        total = jnp.sum(weights, axis=-1, keepdims=True)
        numer = jnp.dot(
            weights.astype(jnp.bfloat16), value_ref[...], preferred_element_type=jnp.float32
        )
        first = slots * rows + g * local
        out_ref[:, first : first + 2 * local, :] = side_by_side(numer[:samples], numer[samples:])
        top = top * SCALE
        peaks = jnp.where(lane == g, top[:samples], peaks)
        peaks = jnp.where(lane == g + 1, top[samples:], peaks)
        sums = jnp.where(lane == g, total[:samples], sums)
        sums = jnp.where(lane == g + 1, total[samples:], sums)

    stats = jnp.zeros((samples, 128), jnp.float32)
    for place, term in enumerate(split3(peaks) + split3(sums)):
        term = term.astype(jnp.float32)
        stats = stats + (pltpu.roll(term, place * GROUP, 1) if place else term)
    first = slots * rows + GROUP * local
    out_ref[:, first:, :] = side_by_side(stats, jnp.zeros_like(stats))


def partial_shared(place, query_rows, pairs, owners):
    samples = query_rows.shape[0]
    pieces, rows, features = pairs.shape
    tokens = pieces * rows // 2
    sent = pieces // owners * rows + (GROUP + 2) * (samples // owners)
    return pl.pallas_call(
        shared_kernel,
        out_shape=jax.ShapeDtypeStruct((owners, sent, features), jnp.bfloat16),
        in_specs=[
            pl.BlockSpec(memory_space=pltpu.SMEM),
            pl.BlockSpec(memory_space=pltpu.VMEM),
            pl.BlockSpec(memory_space=pltpu.VMEM),
        ],
        out_specs=pl.BlockSpec(memory_space=pltpu.VMEM),
        scratch_shapes=[
            pltpu.VMEM((tokens, features), jnp.bfloat16),
            pltpu.VMEM((tokens, features), jnp.bfloat16),
        ],
        compiler_params=pltpu.CompilerParams(vmem_limit_bytes=40 * 1024 * 1024),
        cost_estimate=pl.CostEstimate(
            flops=4 * samples * GROUP * tokens * features,
            bytes_accessed=4 * 1024 * 1024,
            transcendentals=samples * GROUP * tokens,
        ),
    )(place, query_rows, pairs)


def finish_kernel(tile_ref, came_ref, numer_ref, stats_ref, out_ref, pool_ref, sems):
    senders = came_ref.shape[0]
    slots = pool_ref.shape[0]
    local = out_ref.shape[0]
    half = tile_ref.shape[2]
    pool_rows = slots * half * 2
    copies = []
    for sender in range(senders):
        head, part = sender // 2, sender % 2
        copies.append(
            pltpu.make_async_copy(
                tile_ref.at[sender, 0:slots],
                pool_ref.at[
                    :,
                    part * half : (part + 1) * half,
                    :,
                    head * HEAD_FEATURES : (head + 1) * HEAD_FEATURES,
                ],
                sems.at[sender],
            )
        )
        copies[-1].start()

    first = pool_rows + GROUP * local

    def back(x, places):
        return pltpu.roll(x, 128 - places, 1)

    for head in range(KEY_VALUE_HEADS):
        peaks = [stats_ref[head, 0]]
        sums = [stats_ref[head, 1]]
        for part in range(2):
            terms = came_ref[2 * head + part, first : first + 2 * local, :]
            terms = terms.astype(jnp.float32)[:local]
            terms = (terms + back(terms, GROUP)) + back(terms, 2 * GROUP)
            peaks.append(terms)
            sums.append(back(terms, 3 * GROUP))
        peak = jnp.maximum(jnp.maximum(peaks[0], peaks[1]), peaks[2])
        scales = [jnp.exp(p - peak) for p in peaks]
        total = (sums[0] * scales[0] + sums[1] * scales[1]) + sums[2] * scales[2]
        scales = [s / total for s in scales]
        for g in range(0, GROUP, 2):
            rows = slice(g * local, (g + 2) * local)
            numers = [numer_ref[head, rows]] + [
                came_ref[
                    2 * head + part, pool_rows + g * local : pool_rows + (g + 2) * local, :
                ].astype(jnp.float32)
                for part in range(2)
            ]
            for k in range(2):
                mine = [n[k * local : (k + 1) * local] for n in numers]
                by = [s[:, g + k : g + k + 1] for s in scales]
                value = (mine[0] * by[0] + mine[1] * by[1]) + mine[2] * by[2]
                column = (head * GROUP + g + k) * HEAD_FEATURES
                out_ref[:, column : column + HEAD_FEATURES] = value.astype(jnp.bfloat16)

    for copy in copies:
        copy.wait()


def finish(came, numer, stats, local, slots):
    senders, rows, features = came.shape
    half = PAGE_TOKENS // 2
    tiles = came.reshape(senders, rows // (2 * half), half, 2, features)
    return pl.pallas_call(
        finish_kernel,
        out_shape=(
            jax.ShapeDtypeStruct((local, QUERY_HEADS * HEAD_FEATURES), jnp.bfloat16),
            jax.ShapeDtypeStruct(
                (slots, PAGE_TOKENS, 2, KEY_VALUE_HEADS * HEAD_FEATURES), jnp.bfloat16
            ),
        ),
        in_specs=[
            pl.BlockSpec(memory_space=pl.ANY),
            pl.BlockSpec(memory_space=pltpu.VMEM),
            pl.BlockSpec(memory_space=pltpu.VMEM),
            pl.BlockSpec(memory_space=pltpu.VMEM),
        ],
        out_specs=(pl.BlockSpec(memory_space=pltpu.VMEM), pl.BlockSpec(memory_space=pl.ANY)),
        scratch_shapes=[pltpu.SemaphoreType.DMA((senders,))],
        compiler_params=pltpu.CompilerParams(vmem_limit_bytes=32 * 1024 * 1024),
        cost_estimate=pl.CostEstimate(
            flops=6 * local * QUERY_HEADS * HEAD_FEATURES,
            bytes_accessed=4 * 1024 * 1024,
            transcendentals=0,
        ),
    )(tiles, came, numer, stats)


def choose_kernel(match_ref, page_ref, out_ref):
    for instance in range(out_ref.shape[0]):
        page = page_ref[match_ref[instance]]
        for head in range(KEY_VALUE_HEADS):
            out_ref[instance, head] = page[
                :, :, head * HEAD_FEATURES : (head + 1) * HEAD_FEATURES
            ]


def choose(match, pages):
    instances, tokens = pages.shape[:2]
    return pl.pallas_call(
        choose_kernel,
        out_shape=jax.ShapeDtypeStruct(
            (instances, KEY_VALUE_HEADS, tokens, 2, HEAD_FEATURES), pages.dtype
        ),
        in_specs=[
            pl.BlockSpec(memory_space=pltpu.SMEM),
            pl.BlockSpec(memory_space=pltpu.VMEM),
        ],
        out_specs=pl.BlockSpec(memory_space=pltpu.VMEM),
        compiler_params=pltpu.CompilerParams(vmem_limit_bytes=16 * 1024 * 1024),
        cost_estimate=pl.CostEstimate(
            flops=0, bytes_accessed=4 * 1024 * 1024, transcendentals=0
        ),
    )(match, pages)


def gather_queries(local_queries, member, n_samp):
    local = local_queries.shape[0]
    held = local_queries.reshape(local, KEY_VALUE_HEADS, WIDTH).transpose(1, 0, 2)
    for step, place in enumerate((3, 2, 1, 0)):
        bit = (member >> place) & 1
        if place:
            half = held.shape[0] // 2
            kept = lax.dynamic_slice_in_dim(held, bit * half, half, 0)
            sent = lax.dynamic_slice_in_dim(held, (1 - bit) * half, half, 0)
        else:
            kept = sent = held
        pairs = [(i, i ^ (1 << place)) for i in range(n_samp)]
        came = lax.ppermute(sent, "samp", pairs)
        held = jnp.stack(
            [jnp.where(bit == 0, kept, came), jnp.where(bit == 0, came, kept)], axis=1 + step
        )
    return held.reshape(n_samp * local, WIDTH)


def body(n_inst, n_samp, prompt_key_values, match, page_list, queries, sample_key_values, gen_len):
    local_total = queries.shape[1]
    pages_dev = page_list.shape[2]
    half = PAGE_TOKENS // 2
    member = lax.axis_index("samp")
    local_queries = queries[0]

    pages = lax.all_to_all(prompt_key_values, "inst", split_axis=1, concat_axis=0, tiled=True)

    sample_keys = sample_key_values[0, :, :, 0, :]
    sample_values = sample_key_values[0, :, :, 1, :]
    sample_keys, sent_queries = lax.optimization_barrier((sample_keys, local_queries))
    head_queries = gather_queries(sent_queries, member, n_samp)
    live_mask = jnp.arange(sample_keys.shape[1], dtype=jnp.int32)[None, :] < gen_len[0][:, None]
    own_peak, own_sum, own_numer = partial_own(local_queries, sample_keys, sample_values, live_mask)
    own_stats = jnp.stack([own_peak.transpose(1, 0, 2), own_sum.transpose(1, 0, 2)], axis=1)
    own_stats = jnp.pad(own_stats, ((0, 0), (0, 0), (0, 0), (0, 128 - GROUP)))
    own_numer = own_numer.transpose(1, 2, 0, 3).reshape(
        KEY_VALUE_HEADS, GROUP * local_total, HEAD_FEATURES
    )

    listed = page_list[0].reshape(-1)
    place = (listed % pages_dev) * n_samp + listed // pages_dev

    chosen = choose(match, pages).reshape(n_inst * n_samp, half * 2, HEAD_FEATURES)
    pairs = lax.all_to_all(chosen, ("inst", "samp"), split_axis=0, concat_axis=0, tiled=True)
    pairs, place, head_queries, own_stats, own_numer = lax.optimization_barrier(
        (pairs, place, head_queries, own_stats, own_numer)
    )

    sent = partial_shared(place, head_queries, pairs, n_samp)
    came = lax.all_to_all(sent, "samp", split_axis=0, concat_axis=0, tiled=True)
    attended, page_pool = finish(came, own_numer, own_stats, local_total, pages_dev)
    return (attended[None], page_pool[None])


def solution(mesh):
    in_specs = (
        P("inst", "samp", None, None),
        P(),
        P("inst", None, None),
        P("inst", "samp", None),
        P("inst", "samp", None, None, None),
        P("inst", "samp"),
    )
    out_specs = (P("inst", "samp", None), P("inst", "samp", None, None, None))
    step = functools.partial(body, mesh.shape["inst"], mesh.shape["samp"])
    return jax.shard_map(step, mesh=mesh, in_specs=in_specs, out_specs=out_specs, check_vma=False)
```

```python
import functools
import math

import jax
import jax.numpy as jnp
from jax import lax
from jax.experimental import pallas as pl
from jax.experimental.pallas import tpu as pltpu
from jax.sharding import PartitionSpec as P

QUERY_HEADS = 96
KEY_VALUE_HEADS = 8
HEAD_FEATURES = 128
PAGE_TOKENS = 16
GROUP = QUERY_HEADS // KEY_VALUE_HEADS
WIDTH = GROUP * HEAD_FEATURES
SCALE = HEAD_FEATURES ** (-0.5)


def own_kernel(head_at, length_ref, query_ref, cache_ref, numer_ref, stats_ref):
    samples, positions = cache_ref.shape[:2]
    factor = SCALE * math.log2(math.e)
    rows = query_ref.shape[2]
    column = lax.broadcasted_iota(jnp.int32, (rows, 2 * positions), 1)
    diagonal = lax.broadcasted_iota(jnp.int32, (rows, 128), 0) == lax.broadcasted_iota(
        jnp.int32, (rows, 128), 1
    )

    def across(x):
        return jnp.sum(jnp.where(diagonal, x, 0.0), axis=0, keepdims=True)

    def one_head(head, carry):
        start = pl.multiple_of(head * HEAD_FEATURES, HEAD_FEATURES)
        for sample in range(samples):
            live = (column % 2 == 0) & (column < 2 * length_ref[sample])
            both = cache_ref[sample, :, :, pl.ds(start, HEAD_FEATURES)].reshape(
                2 * positions, HEAD_FEATURES
            )
            scores = lax.dot_general(
                query_ref[sample, head_at + head], both, (((1,), (1,)), ((), ())),
                preferred_element_type=jnp.float32,
            )
            top = jnp.max(jnp.where(live, scores, -jnp.inf), axis=-1, keepdims=True)
            weights = jnp.where(live, jnp.exp2((scores - top) * factor), 0.0)
            total = jnp.sum(weights, axis=-1, keepdims=True)
            onto_values = pltpu.roll(weights, 1, 1).astype(jnp.bfloat16)
            numer = jnp.dot(onto_values, both, preferred_element_type=jnp.float32)
            numer_ref[head, :, sample, :] = numer[:GROUP]
            stats_ref[head, 0, sample : sample + 1, :] = across(top * SCALE)
            stats_ref[head, 1, sample : sample + 1, :] = across(total)
        return carry

    lax.fori_loop(0, numer_ref.shape[0], one_head, 0)


def partial_own(lengths, grouped, cache, which, parts):
    samples, positions = cache.shape[:2]
    heads = KEY_VALUE_HEADS // parts
    block = (samples, positions, 2, heads * HEAD_FEATURES)
    return pl.pallas_call(
        functools.partial(own_kernel, which * heads),
        grid=(1,),
        out_shape=(
            jax.ShapeDtypeStruct((heads, GROUP, samples, HEAD_FEATURES), jnp.float32),
            jax.ShapeDtypeStruct((heads, 2, samples, 128), jnp.float32),
        ),
        in_specs=[
            pl.BlockSpec(memory_space=pltpu.SMEM),
            pl.BlockSpec(memory_space=pltpu.VMEM),
            pl.BlockSpec(block, lambda i: (0, 0, 0, which)),
        ],
        out_specs=(
            pl.BlockSpec(memory_space=pltpu.VMEM),
            pl.BlockSpec(memory_space=pltpu.VMEM),
        ),
        compiler_params=pltpu.CompilerParams(vmem_limit_bytes=24 * 1024 * 1024),
        cost_estimate=pl.CostEstimate(flops=0, bytes_accessed=65536, transcendentals=0),
    )(lengths, grouped, cache)


def split3(x):
    high = x.astype(jnp.bfloat16)
    rest = x - high.astype(jnp.float32)
    middle = rest.astype(jnp.bfloat16)
    low = (rest - middle.astype(jnp.float32)).astype(jnp.bfloat16)
    return high, middle, low


def shared_kernel(place_ref, query_ref, pair_ref, out_ref, key_ref, value_ref):
    pieces = pair_ref.shape[0]
    samples = query_ref.shape[0]
    owners, rows = out_ref.shape[0], pair_ref.shape[1]
    slots = pieces // owners
    local = samples // owners

    row = lax.broadcasted_iota(jnp.int32, (256, 256), 0)
    column = lax.broadcasted_iota(jnp.int32, (256, 256), 1)
    wanted = jnp.where(row < 128, 2 * row, 2 * (row - 128) + 1)
    pick = jnp.where(column == wanted, 1.0, 0.0).astype(jnp.bfloat16)
    for step in range(pieces // 16):
        both = pair_ref[step * 16 : (step + 1) * 16].reshape(256, HEAD_FEATURES)
        apart = jnp.dot(pick, both, preferred_element_type=jnp.float32).astype(jnp.bfloat16)
        key_ref[step * 128 : (step + 1) * 128, :] = apart[:128]
        value_ref[step * 128 : (step + 1) * 128, :] = apart[128:]
        for n in range(step * 16, (step + 1) * 16):
            row = n % slots * rows
            out_ref[n // slots, row : row + rows, :] = pair_ref[place_ref[n]]

    factor = SCALE * math.log2(math.e)
    lane = lax.broadcasted_iota(jnp.int32, (samples, 128), 1)
    peaks = jnp.zeros((samples, 128), jnp.float32)
    sums = jnp.zeros((samples, 128), jnp.float32)

    def side_by_side(low, high):
        low = low.reshape(owners, local, HEAD_FEATURES)
        high = high.reshape(owners, local, HEAD_FEATURES)
        return jnp.concatenate([low, high], axis=1).astype(jnp.bfloat16)

    for g in range(0, GROUP, 2):
        query = jnp.concatenate(
            [
                query_ref[:, g * HEAD_FEATURES : (g + 1) * HEAD_FEATURES],
                query_ref[:, (g + 1) * HEAD_FEATURES : (g + 2) * HEAD_FEATURES],
            ],
            axis=0,
        )
        scores = lax.dot_general(
            query, key_ref[...], (((1,), (1,)), ((), ())), preferred_element_type=jnp.float32
        )
        top = jnp.max(scores, axis=-1, keepdims=True)
        weights = jnp.exp2((scores - top) * factor)
        total = jnp.sum(weights, axis=-1, keepdims=True)
        numer = jnp.dot(
            weights.astype(jnp.bfloat16), value_ref[...], preferred_element_type=jnp.float32
        )
        first = slots * rows + g * local
        out_ref[:, first : first + 2 * local, :] = side_by_side(numer[:samples], numer[samples:])
        top = top * SCALE
        peaks = jnp.where(lane == g, top[:samples], peaks)
        peaks = jnp.where(lane == g + 1, top[samples:], peaks)
        sums = jnp.where(lane == g, total[:samples], sums)
        sums = jnp.where(lane == g + 1, total[samples:], sums)

    stats = jnp.zeros((samples, 128), jnp.float32)
    for place, term in enumerate(split3(peaks) + split3(sums)):
        term = term.astype(jnp.float32)
        stats = stats + (pltpu.roll(term, place * GROUP, 1) if place else term)
    first = slots * rows + GROUP * local
    out_ref[:, first:, :] = side_by_side(stats, jnp.zeros_like(stats))


def partial_shared(place, query_rows, pairs, owners):
    samples = query_rows.shape[0]
    pieces, rows, features = pairs.shape
    tokens = pieces * rows // 2
    sent = pieces // owners * rows + (GROUP + 2) * (samples // owners)
    return pl.pallas_call(
        shared_kernel,
        out_shape=jax.ShapeDtypeStruct((owners, sent, features), jnp.bfloat16),
        in_specs=[
            pl.BlockSpec(memory_space=pltpu.SMEM),
            pl.BlockSpec(memory_space=pltpu.VMEM),
            pl.BlockSpec(memory_space=pltpu.VMEM),
        ],
        out_specs=pl.BlockSpec(memory_space=pltpu.VMEM),
        scratch_shapes=[
            pltpu.VMEM((tokens, features), jnp.bfloat16),
            pltpu.VMEM((tokens, features), jnp.bfloat16),
        ],
        compiler_params=pltpu.CompilerParams(vmem_limit_bytes=40 * 1024 * 1024),
        cost_estimate=pl.CostEstimate(
            flops=4 * samples * GROUP * tokens * features,
            bytes_accessed=4 * 1024 * 1024,
            transcendentals=samples * GROUP * tokens,
        ),
    )(place, query_rows, pairs)


def finish_kernel(tile_ref, came_ref, *refs):
    own_refs, (out_ref, pool_ref, sems) = refs[:-3], refs[-3:]
    senders = came_ref.shape[0]
    slots = pool_ref.shape[0]
    local = out_ref.shape[0]
    half = tile_ref.shape[2]
    pool_rows = slots * half * 2
    copies = []
    for sender in range(senders):
        head, part = sender // 2, sender % 2
        copies.append(
            pltpu.make_async_copy(
                tile_ref.at[sender, 0:slots],
                pool_ref.at[
                    :,
                    part * half : (part + 1) * half,
                    :,
                    head * HEAD_FEATURES : (head + 1) * HEAD_FEATURES,
                ],
                sems.at[sender],
            )
        )
        copies[-1].start()

    first = pool_rows + GROUP * local

    def back(x, places):
        return pltpu.roll(x, 128 - places, 1)

    for head in range(KEY_VALUE_HEADS):
        heads = own_refs[0].shape[0]
        numer_ref, stats_ref = own_refs[head // heads * 2 : head // heads * 2 + 2]
        peaks = [stats_ref[head % heads, 0]]
        sums = [stats_ref[head % heads, 1]]
        for part in range(2):
            terms = came_ref[2 * head + part, first : first + 2 * local, :]
            terms = terms.astype(jnp.float32)[:local]
            terms = (terms + back(terms, GROUP)) + back(terms, 2 * GROUP)
            peaks.append(terms)
            sums.append(back(terms, 3 * GROUP))
        peak = jnp.maximum(jnp.maximum(peaks[0], peaks[1]), peaks[2])
        scales = [jnp.exp(p - peak) for p in peaks]
        total = (sums[0] * scales[0] + sums[1] * scales[1]) + sums[2] * scales[2]
        scales = [s / total for s in scales]
        for g in range(0, GROUP, 2):
            rows = slice(g * local, (g + 2) * local)
            numers = [numer_ref[head % heads, g : g + 2].reshape(2 * local, HEAD_FEATURES)] + [
                came_ref[
                    2 * head + part, pool_rows + g * local : pool_rows + (g + 2) * local, :
                ].astype(jnp.float32)
                for part in range(2)
            ]
            for k in range(2):
                mine = [n[k * local : (k + 1) * local] for n in numers]
                by = [s[:, g + k : g + k + 1] for s in scales]
                value = (mine[0] * by[0] + mine[1] * by[1]) + mine[2] * by[2]
                column = (head * GROUP + g + k) * HEAD_FEATURES
                out_ref[:, column : column + HEAD_FEATURES] = value.astype(jnp.bfloat16)

    for copy in copies:
        copy.wait()


def finish(came, own, local, slots):
    senders, rows, features = came.shape
    half = PAGE_TOKENS // 2
    tiles = came.reshape(senders, rows // (2 * half), half, 2, features)
    return pl.pallas_call(
        finish_kernel,
        out_shape=(
            jax.ShapeDtypeStruct((local, QUERY_HEADS * HEAD_FEATURES), jnp.bfloat16),
            jax.ShapeDtypeStruct(
                (slots, PAGE_TOKENS, 2, KEY_VALUE_HEADS * HEAD_FEATURES), jnp.bfloat16
            ),
        ),
        in_specs=[
            pl.BlockSpec(memory_space=pl.ANY),
        ]
        + [pl.BlockSpec(memory_space=pltpu.VMEM)] * (1 + len(own)),
        out_specs=(pl.BlockSpec(memory_space=pltpu.VMEM), pl.BlockSpec(memory_space=pl.ANY)),
        scratch_shapes=[pltpu.SemaphoreType.DMA((senders,))],
        compiler_params=pltpu.CompilerParams(vmem_limit_bytes=32 * 1024 * 1024),
        cost_estimate=pl.CostEstimate(
            flops=6 * local * QUERY_HEADS * HEAD_FEATURES,
            bytes_accessed=4 * 1024 * 1024,
            transcendentals=0,
        ),
    )(tiles, came, *own)


def choose_kernel(match_ref, page_ref, out_ref):
    for instance in range(out_ref.shape[0]):
        page = page_ref[match_ref[instance]]
        for head in range(KEY_VALUE_HEADS):
            out_ref[instance, head] = page[
                :, :, head * HEAD_FEATURES : (head + 1) * HEAD_FEATURES
            ]


def choose(match, pages):
    instances, tokens = pages.shape[:2]
    return pl.pallas_call(
        choose_kernel,
        out_shape=jax.ShapeDtypeStruct(
            (instances, KEY_VALUE_HEADS, tokens, 2, HEAD_FEATURES), pages.dtype
        ),
        in_specs=[
            pl.BlockSpec(memory_space=pltpu.SMEM),
            pl.BlockSpec(memory_space=pltpu.VMEM),
        ],
        out_specs=pl.BlockSpec(memory_space=pltpu.VMEM),
        compiler_params=pltpu.CompilerParams(vmem_limit_bytes=16 * 1024 * 1024),
        cost_estimate=pl.CostEstimate(
            flops=0, bytes_accessed=4 * 1024 * 1024, transcendentals=0
        ),
    )(match, pages)


def exchange(held, member, n_samp, place, axis):
    bit = (member >> place) & 1
    if place:
        half = held.shape[0] // 2
        kept = lax.dynamic_slice_in_dim(held, bit * half, half, 0)
        sent = lax.dynamic_slice_in_dim(held, (1 - bit) * half, half, 0)
    else:
        kept = sent = held
    came = lax.ppermute(sent, "samp", [(i, i ^ (1 << place)) for i in range(n_samp)])
    return jnp.stack(
        [jnp.where(bit == 0, kept, came), jnp.where(bit == 0, came, kept)], axis=axis
    )


def body(n_inst, n_samp, prompt_key_values, match, page_list, queries, sample_key_values, gen_len):
    local_total = queries.shape[1]
    pages_dev = page_list.shape[2]
    half = PAGE_TOKENS // 2
    member = lax.axis_index("samp")
    local_queries = queries[0]

    pages = lax.all_to_all(prompt_key_values, "inst", split_axis=1, concat_axis=0, tiled=True)

    cache = sample_key_values[0]
    grouped = local_queries.reshape(local_total, KEY_VALUE_HEADS, GROUP, HEAD_FEATURES)
    grouped = jnp.pad(grouped, ((0, 0), (0, 0), (0, 16 - GROUP), (0, 0)))
    own = partial_own(gen_len[0], grouped, cache, 0, 2)

    held = local_queries.reshape(local_total, KEY_VALUE_HEADS, WIDTH).transpose(1, 0, 2)
    held = exchange(held, member, n_samp, 3, 1)
    held = exchange(held, member, n_samp, 2, 2)

    listed = page_list[0].reshape(-1)
    place = (listed % pages_dev) * n_samp + listed // pages_dev

    chosen = choose(match, pages).reshape(n_inst * n_samp, half * 2, HEAD_FEATURES)
    chosen, held, grouped, own = lax.optimization_barrier((chosen, held, grouped, own))
    pairs = lax.all_to_all(chosen, ("inst", "samp"), split_axis=0, concat_axis=0, tiled=True)

    own = own + partial_own(gen_len[0], grouped, cache, 1, 2)
    held = exchange(held, member, n_samp, 1, 3)
    held = exchange(held, member, n_samp, 0, 4)
    head_queries = held.reshape(n_samp * local_total, WIDTH)
    pairs, place, head_queries, own = lax.optimization_barrier((pairs, place, head_queries, own))

    sent = partial_shared(place, head_queries, pairs, n_samp)
    came = lax.all_to_all(sent, "samp", split_axis=0, concat_axis=0, tiled=True)
    attended, page_pool = finish(came, own, local_total, pages_dev)
    return (attended[None], page_pool[None])


def solution(mesh):
    in_specs = (
        P("inst", "samp", None, None),
        P(),
        P("inst", None, None),
        P("inst", "samp", None),
        P("inst", "samp", None, None, None),
        P("inst", "samp"),
    )
    out_specs = (P("inst", "samp", None), P("inst", "samp", None, None, None))
    step = functools.partial(body, mesh.shape["inst"], mesh.shape["samp"])
    return jax.shard_map(step, mesh=mesh, in_specs=in_specs, out_specs=out_specs, check_vma=False)
```

```python
import functools
import math

import jax
import jax.numpy as jnp
from jax import lax
from jax.experimental import pallas as pl
from jax.experimental.pallas import tpu as pltpu
from jax.sharding import PartitionSpec as P

QUERY_HEADS = 96
KEY_VALUE_HEADS = 8
HEAD_FEATURES = 128
PAGE_TOKENS = 16
GROUP = QUERY_HEADS // KEY_VALUE_HEADS
WIDTH = GROUP * HEAD_FEATURES
SCALE = HEAD_FEATURES ** (-0.5)


def own_kernel(head_at, length_ref, query_ref, cache_ref, numer_ref, stats_ref):
    samples, positions = cache_ref.shape[:2]
    factor = SCALE * math.log2(math.e)
    rows = query_ref.shape[2]
    column = lax.broadcasted_iota(jnp.int32, (rows, 2 * positions), 1)
    diagonal = lax.broadcasted_iota(jnp.int32, (rows, 128), 0) == lax.broadcasted_iota(
        jnp.int32, (rows, 128), 1
    )

    def across(x):
        return jnp.sum(jnp.where(diagonal, x, 0.0), axis=0, keepdims=True)

    def one_head(head, carry):
        start = pl.multiple_of(head * HEAD_FEATURES, HEAD_FEATURES)
        for sample in range(samples):
            live = (column % 2 == 0) & (column < 2 * length_ref[sample])
            both = cache_ref[sample, :, :, pl.ds(start, HEAD_FEATURES)].reshape(
                2 * positions, HEAD_FEATURES
            )
            scores = lax.dot_general(
                query_ref[sample, head_at + head], both, (((1,), (1,)), ((), ())),
                preferred_element_type=jnp.float32,
            )
            top = jnp.max(jnp.where(live, scores, -jnp.inf), axis=-1, keepdims=True)
            weights = jnp.where(live, jnp.exp2((scores - top) * factor), 0.0)
            total = jnp.sum(weights, axis=-1, keepdims=True)
            onto_values = pltpu.roll(weights, 1, 1).astype(jnp.bfloat16)
            numer = jnp.dot(onto_values, both, preferred_element_type=jnp.float32)
            numer_ref[head, :, sample, :] = numer[:GROUP]
            stats_ref[head, 0, sample : sample + 1, :] = across(top * SCALE)
            stats_ref[head, 1, sample : sample + 1, :] = across(total)
        return carry

    lax.fori_loop(0, numer_ref.shape[0], one_head, 0)


def partial_own(lengths, grouped, cache, which, parts):
    samples, positions = cache.shape[:2]
    heads = KEY_VALUE_HEADS // parts
    block = (samples, positions, 2, heads * HEAD_FEATURES)
    return pl.pallas_call(
        functools.partial(own_kernel, which * heads),
        grid=(1,),
        out_shape=(
            jax.ShapeDtypeStruct((heads, GROUP, samples, HEAD_FEATURES), jnp.float32),
            jax.ShapeDtypeStruct((heads, 2, samples, 128), jnp.float32),
        ),
        in_specs=[
            pl.BlockSpec(memory_space=pltpu.SMEM),
            pl.BlockSpec(memory_space=pltpu.VMEM),
            pl.BlockSpec(block, lambda i: (0, 0, 0, which)),
        ],
        out_specs=(
            pl.BlockSpec(memory_space=pltpu.VMEM),
            pl.BlockSpec(memory_space=pltpu.VMEM),
        ),
        compiler_params=pltpu.CompilerParams(vmem_limit_bytes=24 * 1024 * 1024),
        cost_estimate=pl.CostEstimate(flops=0, bytes_accessed=65536, transcendentals=0),
    )(lengths, grouped, cache)


def split3(x):
    high = x.astype(jnp.bfloat16)
    rest = x - high.astype(jnp.float32)
    middle = rest.astype(jnp.bfloat16)
    low = (rest - middle.astype(jnp.float32)).astype(jnp.bfloat16)
    return high, middle, low


def shared_kernel(place_ref, query_ref, pair_ref, out_ref, key_ref, value_ref):
    pieces = pair_ref.shape[0]
    samples = query_ref.shape[0]
    owners, rows = out_ref.shape[0], pair_ref.shape[1]
    slots = pieces // owners
    local = samples // owners

    row = lax.broadcasted_iota(jnp.int32, (256, 256), 0)
    column = lax.broadcasted_iota(jnp.int32, (256, 256), 1)
    wanted = jnp.where(row < 128, 2 * row, 2 * (row - 128) + 1)
    pick = jnp.where(column == wanted, 1.0, 0.0).astype(jnp.bfloat16)
    for step in range(pieces // 16):
        both = pair_ref[step * 16 : (step + 1) * 16].reshape(256, HEAD_FEATURES)
        apart = jnp.dot(pick, both, preferred_element_type=jnp.float32).astype(jnp.bfloat16)
        key_ref[step * 128 : (step + 1) * 128, :] = apart[:128]
        value_ref[step * 128 : (step + 1) * 128, :] = apart[128:]
        for n in range(step * 16, (step + 1) * 16):
            row = n % slots * rows
            out_ref[n // slots, row : row + rows, :] = pair_ref[place_ref[n]]

    factor = SCALE * math.log2(math.e)
    lane = lax.broadcasted_iota(jnp.int32, (samples, 128), 1)
    peaks = jnp.zeros((samples, 128), jnp.float32)
    sums = jnp.zeros((samples, 128), jnp.float32)

    def side_by_side(low, high):
        low = low.reshape(owners, local, HEAD_FEATURES)
        high = high.reshape(owners, local, HEAD_FEATURES)
        return jnp.concatenate([low, high], axis=1).astype(jnp.bfloat16)

    def scores_of(g):
        query = jnp.concatenate(
            [
                query_ref[:, g * HEAD_FEATURES : (g + 1) * HEAD_FEATURES],
                query_ref[:, (g + 1) * HEAD_FEATURES : (g + 2) * HEAD_FEATURES],
            ],
            axis=0,
        )
        return lax.dot_general(
            query, key_ref[...], (((1,), (1,)), ((), ())), preferred_element_type=jnp.float32
        )

    later = scores_of(0)
    for g in range(0, GROUP, 2):
        scores = later
        if g + 2 < GROUP:
            later = scores_of(g + 2)
        top = jnp.max(scores, axis=-1, keepdims=True)
        weights = jnp.exp2((scores - top) * factor)
        total = jnp.sum(weights, axis=-1, keepdims=True)
        numer = jnp.dot(
            weights.astype(jnp.bfloat16), value_ref[...], preferred_element_type=jnp.float32
        )
        first = slots * rows + g * local
        out_ref[:, first : first + 2 * local, :] = side_by_side(numer[:samples], numer[samples:])
        top = top * SCALE
        peaks = jnp.where(lane == g, top[:samples], peaks)
        peaks = jnp.where(lane == g + 1, top[samples:], peaks)
        sums = jnp.where(lane == g, total[:samples], sums)
        sums = jnp.where(lane == g + 1, total[samples:], sums)

    stats = jnp.zeros((samples, 128), jnp.float32)
    for place, term in enumerate(split3(peaks) + split3(sums)):
        term = term.astype(jnp.float32)
        stats = stats + (pltpu.roll(term, place * GROUP, 1) if place else term)
    first = slots * rows + GROUP * local
    out_ref[:, first:, :] = side_by_side(stats, jnp.zeros_like(stats))


def partial_shared(place, query_rows, pairs, owners):
    samples = query_rows.shape[0]
    pieces, rows, features = pairs.shape
    tokens = pieces * rows // 2
    sent = pieces // owners * rows + (GROUP + 2) * (samples // owners)
    return pl.pallas_call(
        shared_kernel,
        out_shape=jax.ShapeDtypeStruct((owners, sent, features), jnp.bfloat16),
        in_specs=[
            pl.BlockSpec(memory_space=pltpu.SMEM),
            pl.BlockSpec(memory_space=pltpu.VMEM),
            pl.BlockSpec(memory_space=pltpu.VMEM),
        ],
        out_specs=pl.BlockSpec(memory_space=pltpu.VMEM),
        scratch_shapes=[
            pltpu.VMEM((tokens, features), jnp.bfloat16),
            pltpu.VMEM((tokens, features), jnp.bfloat16),
        ],
        compiler_params=pltpu.CompilerParams(vmem_limit_bytes=40 * 1024 * 1024),
        cost_estimate=pl.CostEstimate(
            flops=4 * samples * GROUP * tokens * features,
            bytes_accessed=4 * 1024 * 1024,
            transcendentals=samples * GROUP * tokens,
        ),
    )(place, query_rows, pairs)


def finish_kernel(tile_ref, came_ref, *refs):
    own_refs, (out_ref, pool_ref, sems) = refs[:-3], refs[-3:]
    senders = came_ref.shape[0]
    slots = pool_ref.shape[0]
    local = out_ref.shape[0]
    half = tile_ref.shape[2]
    pool_rows = slots * half * 2
    copies = []
    for sender in range(senders):
        head, part = sender // 2, sender % 2
        copies.append(
            pltpu.make_async_copy(
                tile_ref.at[sender, 0:slots],
                pool_ref.at[
                    :,
                    part * half : (part + 1) * half,
                    :,
                    head * HEAD_FEATURES : (head + 1) * HEAD_FEATURES,
                ],
                sems.at[sender],
            )
        )
        copies[-1].start()

    first = pool_rows + GROUP * local

    def back(x, places):
        return pltpu.roll(x, 128 - places, 1)

    for head in range(KEY_VALUE_HEADS):
        heads = own_refs[0].shape[0]
        numer_ref, stats_ref = own_refs[head // heads * 2 : head // heads * 2 + 2]
        peaks = [stats_ref[head % heads, 0]]
        sums = [stats_ref[head % heads, 1]]
        for part in range(2):
            terms = came_ref[2 * head + part, first : first + 2 * local, :]
            terms = terms.astype(jnp.float32)[:local]
            terms = (terms + back(terms, GROUP)) + back(terms, 2 * GROUP)
            peaks.append(terms)
            sums.append(back(terms, 3 * GROUP))
        peak = jnp.maximum(jnp.maximum(peaks[0], peaks[1]), peaks[2])
        scales = [jnp.exp(p - peak) for p in peaks]
        total = (sums[0] * scales[0] + sums[1] * scales[1]) + sums[2] * scales[2]
        scales = [s / total for s in scales]
        for g in range(0, GROUP, 2):
            rows = slice(g * local, (g + 2) * local)
            numers = [numer_ref[head % heads, g : g + 2].reshape(2 * local, HEAD_FEATURES)] + [
                came_ref[
                    2 * head + part, pool_rows + g * local : pool_rows + (g + 2) * local, :
                ].astype(jnp.float32)
                for part in range(2)
            ]
            for k in range(2):
                mine = [n[k * local : (k + 1) * local] for n in numers]
                by = [s[:, g + k : g + k + 1] for s in scales]
                value = (mine[0] * by[0] + mine[1] * by[1]) + mine[2] * by[2]
                column = (head * GROUP + g + k) * HEAD_FEATURES
                out_ref[:, column : column + HEAD_FEATURES] = value.astype(jnp.bfloat16)

    for copy in copies:
        copy.wait()


def finish(came, own, local, slots):
    senders, rows, features = came.shape
    half = PAGE_TOKENS // 2
    tiles = came.reshape(senders, rows // (2 * half), half, 2, features)
    return pl.pallas_call(
        finish_kernel,
        out_shape=(
            jax.ShapeDtypeStruct((local, QUERY_HEADS * HEAD_FEATURES), jnp.bfloat16),
            jax.ShapeDtypeStruct(
                (slots, PAGE_TOKENS, 2, KEY_VALUE_HEADS * HEAD_FEATURES), jnp.bfloat16
            ),
        ),
        in_specs=[
            pl.BlockSpec(memory_space=pl.ANY),
        ]
        + [pl.BlockSpec(memory_space=pltpu.VMEM)] * (1 + len(own)),
        out_specs=(pl.BlockSpec(memory_space=pltpu.VMEM), pl.BlockSpec(memory_space=pl.ANY)),
        scratch_shapes=[pltpu.SemaphoreType.DMA((senders,))],
        compiler_params=pltpu.CompilerParams(vmem_limit_bytes=32 * 1024 * 1024),
        cost_estimate=pl.CostEstimate(
            flops=6 * local * QUERY_HEADS * HEAD_FEATURES,
            bytes_accessed=4 * 1024 * 1024,
            transcendentals=0,
        ),
    )(tiles, came, *own)


def choose_kernel(match_ref, page_ref, out_ref):
    for instance in range(out_ref.shape[0]):
        page = page_ref[match_ref[instance]]
        for head in range(KEY_VALUE_HEADS):
            out_ref[instance, head] = page[
                :, :, head * HEAD_FEATURES : (head + 1) * HEAD_FEATURES
            ]


def choose(match, pages):
    instances, tokens = pages.shape[:2]
    return pl.pallas_call(
        choose_kernel,
        out_shape=jax.ShapeDtypeStruct(
            (instances, KEY_VALUE_HEADS, tokens, 2, HEAD_FEATURES), pages.dtype
        ),
        in_specs=[
            pl.BlockSpec(memory_space=pltpu.SMEM),
            pl.BlockSpec(memory_space=pltpu.VMEM),
        ],
        out_specs=pl.BlockSpec(memory_space=pltpu.VMEM),
        compiler_params=pltpu.CompilerParams(vmem_limit_bytes=16 * 1024 * 1024),
        cost_estimate=pl.CostEstimate(
            flops=0, bytes_accessed=4 * 1024 * 1024, transcendentals=0
        ),
    )(match, pages)


def exchange(held, member, n_samp, place, axis):
    bit = (member >> place) & 1
    if place:
        half = held.shape[0] // 2
        kept = lax.dynamic_slice_in_dim(held, bit * half, half, 0)
        sent = lax.dynamic_slice_in_dim(held, (1 - bit) * half, half, 0)
    else:
        kept = sent = held
    came = lax.ppermute(sent, "samp", [(i, i ^ (1 << place)) for i in range(n_samp)])
    return jnp.stack(
        [jnp.where(bit == 0, kept, came), jnp.where(bit == 0, came, kept)], axis=axis
    )


def body(n_inst, n_samp, prompt_key_values, match, page_list, queries, sample_key_values, gen_len):
    local_total = queries.shape[1]
    pages_dev = page_list.shape[2]
    half = PAGE_TOKENS // 2
    member = lax.axis_index("samp")
    local_queries = queries[0]

    pages = lax.all_to_all(prompt_key_values, "inst", split_axis=1, concat_axis=0, tiled=True)

    cache = sample_key_values[0]
    grouped = local_queries.reshape(local_total, KEY_VALUE_HEADS, GROUP, HEAD_FEATURES)
    grouped = jnp.pad(grouped, ((0, 0), (0, 0), (0, 16 - GROUP), (0, 0)))
    own = partial_own(gen_len[0], grouped, cache, 0, 2)

    held = local_queries.reshape(local_total, KEY_VALUE_HEADS, WIDTH).transpose(1, 0, 2)
    held = exchange(held, member, n_samp, 3, 1)
    held = exchange(held, member, n_samp, 2, 2)

    listed = page_list[0].reshape(-1)
    place = (listed % pages_dev) * n_samp + listed // pages_dev

    chosen = choose(match, pages).reshape(n_inst * n_samp, half * 2, HEAD_FEATURES)
    chosen, held, grouped, own = lax.optimization_barrier((chosen, held, grouped, own))
    pairs = lax.all_to_all(chosen, ("inst", "samp"), split_axis=0, concat_axis=0, tiled=True)

    own = own + partial_own(gen_len[0], grouped, cache, 1, 2)
    held = exchange(held, member, n_samp, 1, 3)
    held = exchange(held, member, n_samp, 0, 4)
    head_queries = held.reshape(n_samp * local_total, WIDTH)
    pairs, place, head_queries, own = lax.optimization_barrier((pairs, place, head_queries, own))

    sent = partial_shared(place, head_queries, pairs, n_samp)
    came = lax.all_to_all(sent, "samp", split_axis=0, concat_axis=0, tiled=True)
    attended, page_pool = finish(came, own, local_total, pages_dev)
    return (attended[None], page_pool[None])


def solution(mesh):
    in_specs = (
        P("inst", "samp", None, None),
        P(),
        P("inst", None, None),
        P("inst", "samp", None),
        P("inst", "samp", None, None, None),
        P("inst", "samp"),
    )
    out_specs = (P("inst", "samp", None), P("inst", "samp", None, None, None))
    step = functools.partial(body, mesh.shape["inst"], mesh.shape["samp"])
    return jax.shard_map(step, mesh=mesh, in_specs=in_specs, out_specs=out_specs, check_vma=False)
```

```python
import functools
import math

import jax
import jax.numpy as jnp
from jax import lax
from jax.experimental import pallas as pl
from jax.experimental.pallas import tpu as pltpu
from jax.sharding import PartitionSpec as P

QUERY_HEADS = 96
KEY_VALUE_HEADS = 8
HEAD_FEATURES = 128
PAGE_TOKENS = 16
GROUP = QUERY_HEADS // KEY_VALUE_HEADS
WIDTH = GROUP * HEAD_FEATURES
SCALE = HEAD_FEATURES ** (-0.5)


def own_kernel(head_at, length_ref, query_ref, cache_ref, numer_ref, stats_ref):
    samples, positions = cache_ref.shape[:2]
    factor = SCALE * math.log2(math.e)
    rows = query_ref.shape[2]
    column = lax.broadcasted_iota(jnp.int32, (rows, 2 * positions), 1)
    diagonal = lax.broadcasted_iota(jnp.int32, (rows, 128), 0) == lax.broadcasted_iota(
        jnp.int32, (rows, 128), 1
    )

    def across(x):
        return jnp.sum(jnp.where(diagonal, x, 0.0), axis=0, keepdims=True)

    def one_head(head, carry):
        start = pl.multiple_of(head * HEAD_FEATURES, HEAD_FEATURES)
        for sample in range(samples):
            live = (column % 2 == 0) & (column < 2 * length_ref[sample])
            both = cache_ref[sample, :, :, pl.ds(start, HEAD_FEATURES)].reshape(
                2 * positions, HEAD_FEATURES
            )
            scores = lax.dot_general(
                query_ref[sample, head_at + head], both, (((1,), (1,)), ((), ())),
                preferred_element_type=jnp.float32,
            )
            top = jnp.max(jnp.where(live, scores, -jnp.inf), axis=-1, keepdims=True)
            weights = jnp.where(live, jnp.exp2((scores - top) * factor), 0.0)
            total = jnp.sum(weights, axis=-1, keepdims=True)
            onto_values = pltpu.roll(weights, 1, 1).astype(jnp.bfloat16)
            numer = jnp.dot(onto_values, both, preferred_element_type=jnp.float32)
            numer_ref[head, :, sample, :] = numer[:GROUP]
            stats_ref[head, 0, sample : sample + 1, :] = across(top * SCALE)
            stats_ref[head, 1, sample : sample + 1, :] = across(total)
        return carry

    lax.fori_loop(0, numer_ref.shape[0], one_head, 0)


def partial_own(lengths, grouped, cache, which, parts):
    samples, positions = cache.shape[:2]
    heads = KEY_VALUE_HEADS // parts
    block = (samples, positions, 2, heads * HEAD_FEATURES)
    return pl.pallas_call(
        functools.partial(own_kernel, which * heads),
        grid=(1,),
        out_shape=(
            jax.ShapeDtypeStruct((heads, GROUP, samples, HEAD_FEATURES), jnp.float32),
            jax.ShapeDtypeStruct((heads, 2, samples, 128), jnp.float32),
        ),
        in_specs=[
            pl.BlockSpec(memory_space=pltpu.SMEM),
            pl.BlockSpec(memory_space=pltpu.VMEM),
            pl.BlockSpec(block, lambda i: (0, 0, 0, which)),
        ],
        out_specs=(
            pl.BlockSpec(memory_space=pltpu.VMEM),
            pl.BlockSpec(memory_space=pltpu.VMEM),
        ),
        compiler_params=pltpu.CompilerParams(vmem_limit_bytes=24 * 1024 * 1024),
        cost_estimate=pl.CostEstimate(flops=0, bytes_accessed=65536, transcendentals=0),
    )(lengths, grouped, cache)


def split3(x):
    high = x.astype(jnp.bfloat16)
    rest = x - high.astype(jnp.float32)
    middle = rest.astype(jnp.bfloat16)
    low = (rest - middle.astype(jnp.float32)).astype(jnp.bfloat16)
    return high, middle, low


def shared_kernel(place_ref, query_ref, pair_ref, out_ref, key_ref, value_ref):
    pieces = pair_ref.shape[0]
    samples = query_ref.shape[0]
    owners, rows = out_ref.shape[0], pair_ref.shape[1]
    slots = pieces // owners
    local = samples // owners

    row = lax.broadcasted_iota(jnp.int32, (256, 256), 0)
    column = lax.broadcasted_iota(jnp.int32, (256, 256), 1)
    wanted = jnp.where(row < 128, 2 * row, 2 * (row - 128) + 1)
    pick = jnp.where(column == wanted, 1.0, 0.0).astype(jnp.bfloat16)
    for step in range(pieces // 16):
        both = pair_ref[step * 16 : (step + 1) * 16].reshape(256, HEAD_FEATURES)
        apart = jnp.dot(pick, both, preferred_element_type=jnp.float32).astype(jnp.bfloat16)
        key_ref[step * 128 : (step + 1) * 128, :] = apart[:128]
        value_ref[step * 128 : (step + 1) * 128, :] = apart[128:]
        for n in range(step * 16, (step + 1) * 16):
            row = n % slots * rows
            out_ref[n // slots, row : row + rows, :] = pair_ref[place_ref[n]]

    factor = SCALE * math.log2(math.e)
    lane = lax.broadcasted_iota(jnp.int32, (samples, 128), 1)
    peaks = jnp.zeros((samples, 128), jnp.float32)
    sums = jnp.zeros((samples, 128), jnp.float32)

    def side_by_side(low, high):
        low = low.reshape(owners, local, HEAD_FEATURES)
        high = high.reshape(owners, local, HEAD_FEATURES)
        return jnp.concatenate([low, high], axis=1).astype(jnp.bfloat16)

    def scores_of(g):
        query = jnp.concatenate(
            [
                query_ref[:, g * HEAD_FEATURES : (g + 1) * HEAD_FEATURES],
                query_ref[:, (g + 1) * HEAD_FEATURES : (g + 2) * HEAD_FEATURES],
            ],
            axis=0,
        )
        return lax.dot_general(
            query, key_ref[...], (((1,), (1,)), ((), ())), preferred_element_type=jnp.float32
        )

    later = scores_of(0)
    for g in range(0, GROUP, 2):
        scores = later
        if g + 2 < GROUP:
            later = scores_of(g + 2)
        top = jnp.max(scores, axis=-1, keepdims=True)
        weights = jnp.exp2((scores - top) * factor)
        total = jnp.sum(weights, axis=-1, keepdims=True)
        numer = jnp.dot(
            weights.astype(jnp.bfloat16), value_ref[...], preferred_element_type=jnp.float32
        )
        first = slots * rows + g * local
        out_ref[:, first : first + 2 * local, :] = side_by_side(numer[:samples], numer[samples:])
        top = top * SCALE
        peaks = jnp.where(lane == g, top[:samples], peaks)
        peaks = jnp.where(lane == g + 1, top[samples:], peaks)
        sums = jnp.where(lane == g, total[:samples], sums)
        sums = jnp.where(lane == g + 1, total[samples:], sums)

    stats = jnp.zeros((samples, 128), jnp.float32)
    for place, term in enumerate(split3(peaks) + split3(sums)):
        term = term.astype(jnp.float32)
        stats = stats + (pltpu.roll(term, place * GROUP, 1) if place else term)
    first = slots * rows + GROUP * local
    out_ref[:, first:, :] = side_by_side(stats, jnp.zeros_like(stats))


def partial_shared(place, query_rows, pairs, owners):
    samples = query_rows.shape[0]
    pieces, rows, features = pairs.shape
    tokens = pieces * rows // 2
    sent = pieces // owners * rows + (GROUP + 2) * (samples // owners)
    return pl.pallas_call(
        shared_kernel,
        out_shape=jax.ShapeDtypeStruct((owners, sent, features), jnp.bfloat16),
        in_specs=[
            pl.BlockSpec(memory_space=pltpu.SMEM),
            pl.BlockSpec(memory_space=pltpu.VMEM),
            pl.BlockSpec(memory_space=pltpu.VMEM),
        ],
        out_specs=pl.BlockSpec(memory_space=pltpu.VMEM),
        scratch_shapes=[
            pltpu.VMEM((tokens, features), jnp.bfloat16),
            pltpu.VMEM((tokens, features), jnp.bfloat16),
        ],
        compiler_params=pltpu.CompilerParams(vmem_limit_bytes=40 * 1024 * 1024),
        cost_estimate=pl.CostEstimate(
            flops=4 * samples * GROUP * tokens * features,
            bytes_accessed=4 * 1024 * 1024,
            transcendentals=samples * GROUP * tokens,
        ),
    )(place, query_rows, pairs)


def finish_kernel(tile_ref, came_ref, *refs):
    own_refs, (out_ref, pool_ref, sems) = refs[:-3], refs[-3:]
    senders = came_ref.shape[0]
    slots = pool_ref.shape[0]
    local = out_ref.shape[0]
    half = tile_ref.shape[2]
    pool_rows = slots * half * 2
    copies = []
    for sender in range(senders):
        head, part = sender // 2, sender % 2
        copies.append(
            pltpu.make_async_copy(
                tile_ref.at[sender, 0:slots],
                pool_ref.at[
                    :,
                    part * half : (part + 1) * half,
                    :,
                    head * HEAD_FEATURES : (head + 1) * HEAD_FEATURES,
                ],
                sems.at[sender],
            )
        )
        copies[-1].start()

    first = pool_rows + GROUP * local

    def back(x, places):
        return pltpu.roll(x, 128 - places, 1)

    heads = own_refs[0].shape[0]
    stacked = [
        jnp.concatenate([ref[...].reshape(heads, 2, local, 128)[:, i] for ref in own_refs[1::2]])
        for i in range(2)
    ]
    peaks = [stacked[0].reshape(-1, 128)]
    sums = [stacked[1].reshape(-1, 128)]
    for part in range(2):
        terms = came_ref[part::2, first : first + 2 * local, :].astype(jnp.float32)
        terms = terms[:, :local].reshape(-1, 128)
        terms = (terms + back(terms, GROUP)) + back(terms, 2 * GROUP)
        peaks.append(terms)
        sums.append(back(terms, 3 * GROUP))
    peak = jnp.maximum(jnp.maximum(peaks[0], peaks[1]), peaks[2])
    scales = [jnp.exp(p - peak) for p in peaks]
    total = (sums[0] * scales[0] + sums[1] * scales[1]) + sums[2] * scales[2]
    scales = [s / total for s in scales]

    for head in range(KEY_VALUE_HEADS):
        numer_ref = own_refs[head // heads * 2]
        mine_at = slice(head * local, (head + 1) * local)
        for g in range(0, GROUP, 2):
            rows = slice(g * local, (g + 2) * local)
            numers = [numer_ref[head % heads, g : g + 2].reshape(2 * local, HEAD_FEATURES)] + [
                came_ref[
                    2 * head + part, pool_rows + g * local : pool_rows + (g + 2) * local, :
                ].astype(jnp.float32)
                for part in range(2)
            ]
            for k in range(2):
                mine = [n[k * local : (k + 1) * local] for n in numers]
                by = [s[mine_at, g + k : g + k + 1] for s in scales]
                value = (mine[0] * by[0] + mine[1] * by[1]) + mine[2] * by[2]
                column = (head * GROUP + g + k) * HEAD_FEATURES
                out_ref[:, column : column + HEAD_FEATURES] = value.astype(jnp.bfloat16)

    for copy in copies:
        copy.wait()


def finish(came, own, local, slots):
    senders, rows, features = came.shape
    half = PAGE_TOKENS // 2
    tiles = came.reshape(senders, rows // (2 * half), half, 2, features)
    return pl.pallas_call(
        finish_kernel,
        out_shape=(
            jax.ShapeDtypeStruct((local, QUERY_HEADS * HEAD_FEATURES), jnp.bfloat16),
            jax.ShapeDtypeStruct(
                (slots, PAGE_TOKENS, 2, KEY_VALUE_HEADS * HEAD_FEATURES), jnp.bfloat16
            ),
        ),
        in_specs=[
            pl.BlockSpec(memory_space=pl.ANY),
        ]
        + [pl.BlockSpec(memory_space=pltpu.VMEM)] * (1 + len(own)),
        out_specs=(pl.BlockSpec(memory_space=pltpu.VMEM), pl.BlockSpec(memory_space=pl.ANY)),
        scratch_shapes=[pltpu.SemaphoreType.DMA((senders,))],
        compiler_params=pltpu.CompilerParams(vmem_limit_bytes=32 * 1024 * 1024),
        cost_estimate=pl.CostEstimate(
            flops=6 * local * QUERY_HEADS * HEAD_FEATURES,
            bytes_accessed=4 * 1024 * 1024,
            transcendentals=0,
        ),
    )(tiles, came, *own)


def choose_kernel(match_ref, page_ref, out_ref, held_ref, sems):
    copies = []
    for instance in range(out_ref.shape[0]):
        page = page_ref[match_ref[instance]]
        for head in range(KEY_VALUE_HEADS):
            held_ref[instance, head] = page[
                :, :, head * HEAD_FEATURES : (head + 1) * HEAD_FEATURES
            ]
        copies.append(
            pltpu.make_async_copy(held_ref.at[instance], out_ref.at[instance], sems.at[instance])
        )
        copies[-1].start()
    for copy in copies:
        copy.wait()


def choose(match, pages):
    instances, tokens = pages.shape[:2]
    shape = (instances, KEY_VALUE_HEADS, tokens, 2, HEAD_FEATURES)
    return pl.pallas_call(
        choose_kernel,
        out_shape=jax.ShapeDtypeStruct(shape, pages.dtype),
        in_specs=[
            pl.BlockSpec(memory_space=pltpu.SMEM),
            pl.BlockSpec(memory_space=pltpu.VMEM),
        ],
        out_specs=pl.BlockSpec(memory_space=pl.ANY),
        scratch_shapes=[
            pltpu.VMEM(shape, pages.dtype),
            pltpu.SemaphoreType.DMA((instances,)),
        ],
        compiler_params=pltpu.CompilerParams(vmem_limit_bytes=16 * 1024 * 1024),
        cost_estimate=pl.CostEstimate(
            flops=0, bytes_accessed=4 * 1024 * 1024, transcendentals=0
        ),
    )(match, pages)


def exchange(held, member, n_samp, place, axis):
    bit = (member >> place) & 1
    if place:
        half = held.shape[0] // 2
        kept = lax.dynamic_slice_in_dim(held, bit * half, half, 0)
        sent = lax.dynamic_slice_in_dim(held, (1 - bit) * half, half, 0)
    else:
        kept = sent = held
    came = lax.ppermute(sent, "samp", [(i, i ^ (1 << place)) for i in range(n_samp)])
    return jnp.stack(
        [jnp.where(bit == 0, kept, came), jnp.where(bit == 0, came, kept)], axis=axis
    )


def body(n_inst, n_samp, prompt_key_values, match, page_list, queries, sample_key_values, gen_len):
    local_total = queries.shape[1]
    pages_dev = page_list.shape[2]
    half = PAGE_TOKENS // 2
    member = lax.axis_index("samp")
    local_queries = queries[0]

    pages = lax.all_to_all(prompt_key_values, "inst", split_axis=1, concat_axis=0, tiled=True)

    cache = sample_key_values[0]
    grouped = local_queries.reshape(local_total, KEY_VALUE_HEADS, GROUP, HEAD_FEATURES)
    grouped = jnp.pad(grouped, ((0, 0), (0, 0), (0, 16 - GROUP), (0, 0)))
    own = partial_own(gen_len[0], grouped, cache, 0, 2)

    held = local_queries.reshape(local_total, KEY_VALUE_HEADS, WIDTH).transpose(1, 0, 2)
    held = exchange(held, member, n_samp, 3, 1)
    held = exchange(held, member, n_samp, 2, 2)

    listed = page_list[0].reshape(-1)
    place = (listed % pages_dev) * n_samp + listed // pages_dev

    chosen = choose(match, pages).reshape(n_inst * n_samp, half * 2, HEAD_FEATURES)
    chosen, held, grouped, own = lax.optimization_barrier((chosen, held, grouped, own))
    pairs = lax.all_to_all(chosen, ("inst", "samp"), split_axis=0, concat_axis=0, tiled=True)

    own = own + partial_own(gen_len[0], grouped, cache, 1, 2)
    held = exchange(held, member, n_samp, 1, 3)
    held = exchange(held, member, n_samp, 0, 4)
    head_queries = held.reshape(n_samp * local_total, WIDTH)
    pairs, place, head_queries, own = lax.optimization_barrier((pairs, place, head_queries, own))

    sent = partial_shared(place, head_queries, pairs, n_samp)
    came = lax.all_to_all(sent, "samp", split_axis=0, concat_axis=0, tiled=True)
    attended, page_pool = finish(came, own, local_total, pages_dev)
    return (attended[None], page_pool[None])


def solution(mesh):
    in_specs = (
        P("inst", "samp", None, None),
        P(),
        P("inst", None, None),
        P("inst", "samp", None),
        P("inst", "samp", None, None, None),
        P("inst", "samp"),
    )
    out_specs = (P("inst", "samp", None), P("inst", "samp", None, None, None))
    step = functools.partial(body, mesh.shape["inst"], mesh.shape["samp"])
    return jax.shard_map(step, mesh=mesh, in_specs=in_specs, out_specs=out_specs, check_vma=False)
```

```python
import functools
import math

import jax
import jax.numpy as jnp
from jax import lax
from jax.experimental import pallas as pl
from jax.experimental.pallas import tpu as pltpu
from jax.sharding import PartitionSpec as P

QUERY_HEADS = 96
KEY_VALUE_HEADS = 8
HEAD_FEATURES = 128
PAGE_TOKENS = 16
GROUP = QUERY_HEADS // KEY_VALUE_HEADS
WIDTH = GROUP * HEAD_FEATURES
SCALE = HEAD_FEATURES ** (-0.5)


def own_kernel(head_at, length_ref, query_ref, cache_ref, numer_ref, stats_ref):
    samples, positions = cache_ref.shape[:2]
    factor = SCALE * math.log2(math.e)
    rows = query_ref.shape[2]
    column = lax.broadcasted_iota(jnp.int32, (rows, 2 * positions), 1)
    diagonal = lax.broadcasted_iota(jnp.int32, (rows, 128), 0) == lax.broadcasted_iota(
        jnp.int32, (rows, 128), 1
    )

    def across(x):
        return jnp.sum(jnp.where(diagonal, x, 0.0), axis=0, keepdims=True)

    def one_head(head, carry):
        start = pl.multiple_of(head * HEAD_FEATURES, HEAD_FEATURES)
        for sample in range(samples):
            live = (column % 2 == 0) & (column < 2 * length_ref[sample])
            both = cache_ref[sample, :, :, pl.ds(start, HEAD_FEATURES)].reshape(
                2 * positions, HEAD_FEATURES
            )
            scores = lax.dot_general(
                query_ref[sample, head_at + head], both, (((1,), (1,)), ((), ())),
                preferred_element_type=jnp.float32,
            )
            top = jnp.max(jnp.where(live, scores, -jnp.inf), axis=-1, keepdims=True)
            weights = jnp.where(live, jnp.exp2((scores - top) * factor), 0.0)
            total = jnp.sum(weights, axis=-1, keepdims=True)
            onto_values = pltpu.roll(weights, 1, 1).astype(jnp.bfloat16)
            numer = jnp.dot(onto_values, both, preferred_element_type=jnp.float32)
            numer_ref[head, :, sample, :] = numer[:GROUP]
            stats_ref[head, 0, sample : sample + 1, :] = across(top * SCALE)
            stats_ref[head, 1, sample : sample + 1, :] = across(total)
        return carry

    lax.fori_loop(0, numer_ref.shape[0], one_head, 0)


def partial_own(lengths, grouped, cache, which, parts):
    samples, positions = cache.shape[:2]
    heads = KEY_VALUE_HEADS // parts
    block = (samples, positions, 2, heads * HEAD_FEATURES)
    return pl.pallas_call(
        functools.partial(own_kernel, which * heads),
        grid=(1,),
        out_shape=(
            jax.ShapeDtypeStruct((heads, GROUP, samples, HEAD_FEATURES), jnp.float32),
            jax.ShapeDtypeStruct((heads, 2, samples, 128), jnp.float32),
        ),
        in_specs=[
            pl.BlockSpec(memory_space=pltpu.SMEM),
            pl.BlockSpec(memory_space=pltpu.VMEM),
            pl.BlockSpec(block, lambda i: (0, 0, 0, which)),
        ],
        out_specs=(
            pl.BlockSpec(memory_space=pltpu.VMEM),
            pl.BlockSpec(memory_space=pltpu.VMEM),
        ),
        compiler_params=pltpu.CompilerParams(vmem_limit_bytes=24 * 1024 * 1024),
        cost_estimate=pl.CostEstimate(flops=0, bytes_accessed=65536, transcendentals=0),
    )(lengths, grouped, cache)


def split3(x):
    high = x.astype(jnp.bfloat16)
    rest = x - high.astype(jnp.float32)
    middle = rest.astype(jnp.bfloat16)
    low = (rest - middle.astype(jnp.float32)).astype(jnp.bfloat16)
    return high, middle, low


def shared_kernel(place_ref, query_ref, pair_ref, out_ref, key_ref, value_ref):
    pieces = pair_ref.shape[0]
    samples = query_ref.shape[0]
    owners, rows = out_ref.shape[0], pair_ref.shape[1]
    slots = pieces // owners
    local = samples // owners

    row = lax.broadcasted_iota(jnp.int32, (256, 256), 0)
    column = lax.broadcasted_iota(jnp.int32, (256, 256), 1)
    wanted = jnp.where(row < 128, 2 * row, 2 * (row - 128) + 1)
    pick = jnp.where(column == wanted, 1.0, 0.0).astype(jnp.bfloat16)
    for step in range(pieces // 16):
        both = pair_ref[step * 16 : (step + 1) * 16].reshape(256, HEAD_FEATURES)
        apart = jnp.dot(pick, both, preferred_element_type=jnp.float32).astype(jnp.bfloat16)
        key_ref[step * 128 : (step + 1) * 128, :] = apart[:128]
        value_ref[step * 128 : (step + 1) * 128, :] = apart[128:]
        for n in range(step * 16, (step + 1) * 16):
            row = n % slots * rows
            out_ref[n // slots, row : row + rows, :] = pair_ref[place_ref[n]]

    factor = SCALE * math.log2(math.e)
    lane = lax.broadcasted_iota(jnp.int32, (samples, 128), 1)
    peaks = jnp.zeros((samples, 128), jnp.float32)
    sums = jnp.zeros((samples, 128), jnp.float32)

    def side_by_side(low, high):
        low = low.reshape(owners, local, HEAD_FEATURES)
        high = high.reshape(owners, local, HEAD_FEATURES)
        return jnp.concatenate([low, high], axis=1).astype(jnp.bfloat16)

    def scores_of(g):
        query = jnp.concatenate(
            [
                query_ref[:, g * HEAD_FEATURES : (g + 1) * HEAD_FEATURES],
                query_ref[:, (g + 1) * HEAD_FEATURES : (g + 2) * HEAD_FEATURES],
            ],
            axis=0,
        )
        return lax.dot_general(
            query, key_ref[...], (((1,), (1,)), ((), ())), preferred_element_type=jnp.float32
        )

    later = scores_of(0)
    for g in range(0, GROUP, 2):
        scores = later
        if g + 2 < GROUP:
            later = scores_of(g + 2)
        top = jnp.max(scores, axis=-1, keepdims=True)
        weights = jnp.exp2((scores - top) * factor)
        total = jnp.sum(weights, axis=-1, keepdims=True)
        numer = jnp.dot(
            weights.astype(jnp.bfloat16), value_ref[...], preferred_element_type=jnp.float32
        )
        first = slots * rows + g * local
        out_ref[:, first : first + 2 * local, :] = side_by_side(numer[:samples], numer[samples:])
        top = top * SCALE
        peaks = jnp.where(lane == g, top[:samples], peaks)
        peaks = jnp.where(lane == g + 1, top[samples:], peaks)
        sums = jnp.where(lane == g, total[:samples], sums)
        sums = jnp.where(lane == g + 1, total[samples:], sums)

    stats = jnp.zeros((samples, 128), jnp.float32)
    for place, term in enumerate(split3(peaks) + split3(sums)):
        term = term.astype(jnp.float32)
        stats = stats + (pltpu.roll(term, place * GROUP, 1) if place else term)
    first = slots * rows + GROUP * local
    out_ref[:, first:, :] = side_by_side(stats, jnp.zeros_like(stats))


def partial_shared(place, query_rows, pairs, owners):
    samples = query_rows.shape[0]
    pieces, rows, features = pairs.shape
    tokens = pieces * rows // 2
    sent = pieces // owners * rows + (GROUP + 2) * (samples // owners)
    return pl.pallas_call(
        shared_kernel,
        out_shape=jax.ShapeDtypeStruct((owners, sent, features), jnp.bfloat16),
        in_specs=[
            pl.BlockSpec(memory_space=pltpu.SMEM),
            pl.BlockSpec(memory_space=pltpu.VMEM),
            pl.BlockSpec(memory_space=pltpu.VMEM),
        ],
        out_specs=pl.BlockSpec(memory_space=pltpu.VMEM),
        scratch_shapes=[
            pltpu.VMEM((tokens, features), jnp.bfloat16),
            pltpu.VMEM((tokens, features), jnp.bfloat16),
        ],
        compiler_params=pltpu.CompilerParams(vmem_limit_bytes=40 * 1024 * 1024),
        cost_estimate=pl.CostEstimate(
            flops=4 * samples * GROUP * tokens * features,
            bytes_accessed=4 * 1024 * 1024,
            transcendentals=samples * GROUP * tokens,
        ),
    )(place, query_rows, pairs)


def finish_kernel(tile_ref, came_ref, *refs):
    own_refs, (out_ref, pool_ref, sems) = refs[:-3], refs[-3:]
    senders = came_ref.shape[0]
    slots = pool_ref.shape[0]
    local = out_ref.shape[0]
    half = tile_ref.shape[2]
    pool_rows = slots * half * 2
    copies = []
    for sender in range(senders):
        head, part = sender // 2, sender % 2
        copies.append(
            pltpu.make_async_copy(
                tile_ref.at[sender, 0:slots],
                pool_ref.at[
                    :,
                    part * half : (part + 1) * half,
                    :,
                    head * HEAD_FEATURES : (head + 1) * HEAD_FEATURES,
                ],
                sems.at[sender],
            )
        )
        copies[-1].start()

    first = pool_rows + GROUP * local

    def back(x, places):
        return pltpu.roll(x, 128 - places, 1)

    heads = own_refs[0].shape[0]
    stacked = [
        jnp.concatenate([ref[...].reshape(heads, 2, local, 128)[:, i] for ref in own_refs[1::2]])
        for i in range(2)
    ]
    peaks = [stacked[0].reshape(-1, 128)]
    sums = [stacked[1].reshape(-1, 128)]
    for part in range(2):
        terms = came_ref[part::2, first : first + 2 * local, :].astype(jnp.float32)
        terms = terms[:, :local].reshape(-1, 128)
        terms = (terms + back(terms, GROUP)) + back(terms, 2 * GROUP)
        peaks.append(terms)
        sums.append(back(terms, 3 * GROUP))
    peak = jnp.maximum(jnp.maximum(peaks[0], peaks[1]), peaks[2])
    scales = [jnp.exp(p - peak) for p in peaks]
    total = (sums[0] * scales[0] + sums[1] * scales[1]) + sums[2] * scales[2]
    scales = [s / total for s in scales]

    for head in range(KEY_VALUE_HEADS):
        numer_ref = own_refs[head // heads * 2]
        mine_at = slice(head * local, (head + 1) * local)
        for g in range(0, GROUP, 2):
            rows = slice(g * local, (g + 2) * local)
            numers = [numer_ref[head % heads, g : g + 2].reshape(2 * local, HEAD_FEATURES)] + [
                came_ref[
                    2 * head + part, pool_rows + g * local : pool_rows + (g + 2) * local, :
                ].astype(jnp.float32)
                for part in range(2)
            ]
            for k in range(2):
                mine = [n[k * local : (k + 1) * local] for n in numers]
                by = [s[mine_at, g + k : g + k + 1] for s in scales]
                value = (mine[0] * by[0] + mine[1] * by[1]) + mine[2] * by[2]
                column = (head * GROUP + g + k) * HEAD_FEATURES
                out_ref[:, column : column + HEAD_FEATURES] = value.astype(jnp.bfloat16)

    for copy in copies:
        copy.wait()


def finish(came, own, local, slots):
    senders, rows, features = came.shape
    half = PAGE_TOKENS // 2
    tiles = came.reshape(senders, rows // (2 * half), half, 2, features)
    return pl.pallas_call(
        finish_kernel,
        out_shape=(
            jax.ShapeDtypeStruct((local, QUERY_HEADS * HEAD_FEATURES), jnp.bfloat16),
            jax.ShapeDtypeStruct(
                (slots, PAGE_TOKENS, 2, KEY_VALUE_HEADS * HEAD_FEATURES), jnp.bfloat16
            ),
        ),
        in_specs=[
            pl.BlockSpec(memory_space=pl.ANY),
        ]
        + [pl.BlockSpec(memory_space=pltpu.VMEM)] * (1 + len(own)),
        out_specs=(pl.BlockSpec(memory_space=pltpu.VMEM), pl.BlockSpec(memory_space=pl.ANY)),
        scratch_shapes=[pltpu.SemaphoreType.DMA((senders,))],
        compiler_params=pltpu.CompilerParams(vmem_limit_bytes=32 * 1024 * 1024),
        cost_estimate=pl.CostEstimate(
            flops=6 * local * QUERY_HEADS * HEAD_FEATURES,
            bytes_accessed=4 * 1024 * 1024,
            transcendentals=0,
        ),
    )(tiles, came, *own)


def split_kernel(page_ref, out_ref, held_ref, sems):
    copies = []
    for page in range(out_ref.shape[0]):
        rows = page_ref[page]
        for head in range(KEY_VALUE_HEADS):
            held_ref[page, head] = rows[:, :, head * HEAD_FEATURES : (head + 1) * HEAD_FEATURES]
        copies.append(pltpu.make_async_copy(held_ref.at[page], out_ref.at[page], sems.at[page]))
        copies[-1].start()
    for copy in copies:
        copy.wait()


def split_heads(pages):
    count, tokens = pages.shape[:2]
    shape = (count, KEY_VALUE_HEADS, tokens, 2, HEAD_FEATURES)
    return pl.pallas_call(
        split_kernel,
        out_shape=jax.ShapeDtypeStruct(shape, pages.dtype),
        in_specs=[pl.BlockSpec(memory_space=pltpu.VMEM)],
        out_specs=pl.BlockSpec(memory_space=pl.ANY),
        scratch_shapes=[
            pltpu.VMEM(shape, pages.dtype),
            pltpu.SemaphoreType.DMA((count,)),
        ],
        compiler_params=pltpu.CompilerParams(vmem_limit_bytes=16 * 1024 * 1024),
        cost_estimate=pl.CostEstimate(
            flops=0, bytes_accessed=4 * 1024 * 1024, transcendentals=0
        ),
    )(pages)


def exchange(held, member, n_samp, place, axis):
    bit = (member >> place) & 1
    if place:
        half = held.shape[0] // 2
        kept = lax.dynamic_slice_in_dim(held, bit * half, half, 0)
        sent = lax.dynamic_slice_in_dim(held, (1 - bit) * half, half, 0)
    else:
        kept = sent = held
    came = lax.ppermute(sent, "samp", [(i, i ^ (1 << place)) for i in range(n_samp)])
    return jnp.stack(
        [jnp.where(bit == 0, kept, came), jnp.where(bit == 0, came, kept)], axis=axis
    )


def body(n_inst, n_samp, prompt_key_values, match, page_list, queries, sample_key_values, gen_len):
    local_total = queries.shape[1]
    pages_dev = page_list.shape[2]
    half = PAGE_TOKENS // 2
    member = lax.axis_index("samp")
    local_queries = queries[0]

    pages = prompt_key_values.reshape(
        n_inst, PAGE_TOKENS, 2, KEY_VALUE_HEADS * HEAD_FEATURES
    )
    pieces = split_heads(pages).reshape(n_inst * n_samp, half * 2, HEAD_FEATURES)
    spread = lax.all_to_all(pieces, ("inst", "samp"), split_axis=0, concat_axis=0, tiled=True)

    cache = sample_key_values[0]
    grouped = local_queries.reshape(local_total, KEY_VALUE_HEADS, GROUP, HEAD_FEATURES)
    grouped = jnp.pad(grouped, ((0, 0), (0, 0), (0, 16 - GROUP), (0, 0)))
    own = partial_own(gen_len[0], grouped, cache, 0, 2)

    held = local_queries.reshape(local_total, KEY_VALUE_HEADS, WIDTH).transpose(1, 0, 2)
    held = exchange(held, member, n_samp, 3, 1)
    held = exchange(held, member, n_samp, 2, 2)

    listed = page_list[0].reshape(-1)
    place = (listed % pages_dev) * n_samp + listed // pages_dev

    blocks = spread.reshape(n_inst, n_samp * half * 2, HEAD_FEATURES)
    blocks = blocks.at[match].get(mode="promise_in_bounds")
    blocks, held, grouped, own = lax.optimization_barrier((blocks, held, grouped, own))
    pairs = lax.all_to_all(blocks, "inst", split_axis=0, concat_axis=0, tiled=True)
    pairs = pairs.reshape(n_inst * n_samp, half * 2, HEAD_FEATURES)

    held = exchange(held, member, n_samp, 1, 3)
    held = exchange(held, member, n_samp, 0, 4)
    head_queries = held.reshape(n_samp * local_total, WIDTH)
    pairs, place, head_queries = lax.optimization_barrier((pairs, place, head_queries))

    sent = partial_shared(place, head_queries, pairs, n_samp)
    sent, grouped = lax.optimization_barrier((sent, grouped))
    own = own + partial_own(gen_len[0], grouped, cache, 1, 2)
    came = lax.all_to_all(sent, "samp", split_axis=0, concat_axis=0, tiled=True)
    attended, page_pool = finish(came, own, local_total, pages_dev)
    return (attended[None], page_pool[None])


def solution(mesh):
    in_specs = (
        P("inst", "samp", None, None),
        P(),
        P("inst", None, None),
        P("inst", "samp", None),
        P("inst", "samp", None, None, None),
        P("inst", "samp"),
    )
    out_specs = (P("inst", "samp", None), P("inst", "samp", None, None, None))
    step = functools.partial(body, mesh.shape["inst"], mesh.shape["samp"])
    return jax.shard_map(step, mesh=mesh, in_specs=in_specs, out_specs=out_specs, check_vma=False)
```

```python
import functools
import math

import jax
import jax.numpy as jnp
from jax import lax
from jax.experimental import pallas as pl
from jax.experimental.pallas import tpu as pltpu
from jax.sharding import PartitionSpec as P

QUERY_HEADS = 96
KEY_VALUE_HEADS = 8
HEAD_FEATURES = 128
PAGE_TOKENS = 16
GROUP = QUERY_HEADS // KEY_VALUE_HEADS
WIDTH = GROUP * HEAD_FEATURES
SCALE = HEAD_FEATURES ** (-0.5)


def own_kernel(head_at, length_ref, query_ref, cache_ref, numer_ref, stats_ref):
    samples, positions = cache_ref.shape[:2]
    factor = SCALE * math.log2(math.e)
    rows = query_ref.shape[2]
    column = lax.broadcasted_iota(jnp.int32, (rows, 2 * positions), 1)
    diagonal = lax.broadcasted_iota(jnp.int32, (rows, 128), 0) == lax.broadcasted_iota(
        jnp.int32, (rows, 128), 1
    )

    def across(x):
        return jnp.sum(jnp.where(diagonal, x, 0.0), axis=0, keepdims=True)

    def one_head(head, carry):
        start = pl.multiple_of(head * HEAD_FEATURES, HEAD_FEATURES)
        for sample in range(samples):
            live = (column % 2 == 0) & (column < 2 * length_ref[sample])
            both = cache_ref[sample, :, :, pl.ds(start, HEAD_FEATURES)].reshape(
                2 * positions, HEAD_FEATURES
            )
            scores = lax.dot_general(
                query_ref[sample, head_at + head], both, (((1,), (1,)), ((), ())),
                preferred_element_type=jnp.float32,
            )
            top = jnp.max(jnp.where(live, scores, -jnp.inf), axis=-1, keepdims=True)
            weights = jnp.where(live, jnp.exp2((scores - top) * factor), 0.0)
            total = jnp.sum(weights, axis=-1, keepdims=True)
            onto_values = pltpu.roll(weights, 1, 1).astype(jnp.bfloat16)
            numer = jnp.dot(onto_values, both, preferred_element_type=jnp.float32)
            numer_ref[head, :, sample, :] = numer[:GROUP]
            stats_ref[head, 0, sample : sample + 1, :] = across(top * SCALE)
            stats_ref[head, 1, sample : sample + 1, :] = across(total)
        return carry

    lax.fori_loop(0, numer_ref.shape[0], one_head, 0)


def partial_own(lengths, grouped, cache, which, parts):
    samples, positions = cache.shape[:2]
    heads = KEY_VALUE_HEADS // parts
    block = (samples, positions, 2, heads * HEAD_FEATURES)
    return pl.pallas_call(
        functools.partial(own_kernel, which * heads),
        grid=(1,),
        out_shape=(
            jax.ShapeDtypeStruct((heads, GROUP, samples, HEAD_FEATURES), jnp.float32),
            jax.ShapeDtypeStruct((heads, 2, samples, 128), jnp.float32),
        ),
        in_specs=[
            pl.BlockSpec(memory_space=pltpu.SMEM),
            pl.BlockSpec(memory_space=pltpu.VMEM),
            pl.BlockSpec(block, lambda i: (0, 0, 0, which)),
        ],
        out_specs=(
            pl.BlockSpec(memory_space=pltpu.VMEM),
            pl.BlockSpec(memory_space=pltpu.VMEM),
        ),
        compiler_params=pltpu.CompilerParams(vmem_limit_bytes=24 * 1024 * 1024),
        cost_estimate=pl.CostEstimate(flops=0, bytes_accessed=65536, transcendentals=0),
    )(lengths, grouped, cache)


def split3(x):
    high = x.astype(jnp.bfloat16)
    rest = x - high.astype(jnp.float32)
    middle = rest.astype(jnp.bfloat16)
    low = (rest - middle.astype(jnp.float32)).astype(jnp.bfloat16)
    return high, middle, low


def shared_kernel(
    listed_ref, query_ref, pair_ref, out_ref, key_ref, value_ref, wide_ref, place_ref, list_sem
):
    pieces = pair_ref.shape[0]
    samples = query_ref.shape[0]
    owners, rows = out_ref.shape[0], pair_ref.shape[1]
    slots = pieces // owners
    local = samples // owners

    fetch = pltpu.make_async_copy(listed_ref, place_ref, list_sem)
    fetch.start()
    for step in range(pieces // 16):
        wide = step % wide_ref.shape[0]
        both = pair_ref[step * 16 : (step + 1) * 16].reshape(256, HEAD_FEATURES)
        wide_ref[wide] = both.astype(jnp.float32)
        here = slice(step * 128, (step + 1) * 128)
        key_ref[here, :] = wide_ref[wide, pl.ds(0, 128, stride=2), :].astype(jnp.bfloat16)
        value_ref[here, :] = wide_ref[wide, pl.ds(1, 128, stride=2), :].astype(jnp.bfloat16)
    factor = SCALE * math.log2(math.e)
    lane = lax.broadcasted_iota(jnp.int32, (samples, 128), 1)
    peaks = jnp.zeros((samples, 128), jnp.float32)
    sums = jnp.zeros((samples, 128), jnp.float32)

    def side_by_side(low, high):
        low = low.reshape(owners, local, HEAD_FEATURES)
        high = high.reshape(owners, local, HEAD_FEATURES)
        return jnp.concatenate([low, high], axis=1).astype(jnp.bfloat16)

    def scores_of(g):
        query = jnp.concatenate(
            [
                query_ref[:, g * HEAD_FEATURES : (g + 1) * HEAD_FEATURES],
                query_ref[:, (g + 1) * HEAD_FEATURES : (g + 2) * HEAD_FEATURES],
            ],
            axis=0,
        )
        return lax.dot_general(
            query, key_ref[...], (((1,), (1,)), ((), ())), preferred_element_type=jnp.float32
        )

    later = scores_of(0)
    fetch.wait()
    for g in range(0, GROUP, 2):
        scores = later
        if g + 2 < GROUP:
            later = scores_of(g + 2)
        for n in range(g * pieces // GROUP, (g + 2) * pieces // GROUP):
            row = n % slots * rows
            out_ref[n // slots, row : row + rows, :] = pair_ref[place_ref[n]]
        top = jnp.max(scores, axis=-1, keepdims=True)
        weights = jnp.exp2((scores - top) * factor)
        total = jnp.sum(weights, axis=-1, keepdims=True)
        numer = jnp.dot(
            weights.astype(jnp.bfloat16), value_ref[...], preferred_element_type=jnp.float32
        )
        first = slots * rows + g * local
        out_ref[:, first : first + 2 * local, :] = side_by_side(numer[:samples], numer[samples:])
        top = top * SCALE
        peaks = jnp.where(lane == g, top[:samples], peaks)
        peaks = jnp.where(lane == g + 1, top[samples:], peaks)
        sums = jnp.where(lane == g, total[:samples], sums)
        sums = jnp.where(lane == g + 1, total[samples:], sums)

    stats = jnp.zeros((samples, 128), jnp.float32)
    for place, term in enumerate(split3(peaks) + split3(sums)):
        term = term.astype(jnp.float32)
        stats = stats + (pltpu.roll(term, place * GROUP, 1) if place else term)
    first = slots * rows + GROUP * local
    out_ref[:, first:, :] = side_by_side(stats, jnp.zeros_like(stats))


def partial_shared(place, query_rows, pairs, owners):
    samples = query_rows.shape[0]
    pieces, rows, features = pairs.shape
    tokens = pieces * rows // 2
    sent = pieces // owners * rows + (GROUP + 2) * (samples // owners)
    return pl.pallas_call(
        shared_kernel,
        out_shape=jax.ShapeDtypeStruct((owners, sent, features), jnp.bfloat16),
        in_specs=[
            pl.BlockSpec(memory_space=pl.ANY),
            pl.BlockSpec(memory_space=pltpu.VMEM),
            pl.BlockSpec(memory_space=pltpu.VMEM),
        ],
        out_specs=pl.BlockSpec(memory_space=pltpu.VMEM),
        scratch_shapes=[
            pltpu.VMEM((tokens, features), jnp.bfloat16),
            pltpu.VMEM((tokens, features), jnp.bfloat16),
            pltpu.VMEM((4, 256, features), jnp.float32),
            pltpu.SMEM((pieces,), jnp.int32),
            pltpu.SemaphoreType.DMA,
        ],
        compiler_params=pltpu.CompilerParams(vmem_limit_bytes=40 * 1024 * 1024),
        cost_estimate=pl.CostEstimate(
            flops=4 * samples * GROUP * tokens * features,
            bytes_accessed=4 * 1024 * 1024,
            transcendentals=samples * GROUP * tokens,
        ),
    )(place, query_rows, pairs)


def finish_kernel(tile_ref, came_ref, *refs):
    own_refs, (out_ref, pool_ref, sems) = refs[:-3], refs[-3:]
    senders = came_ref.shape[0]
    slots = pool_ref.shape[0]
    local = out_ref.shape[0]
    half = tile_ref.shape[2]
    pool_rows = slots * half * 2
    copies = []
    for sender in range(senders):
        head, part = sender // 2, sender % 2
        copies.append(
            pltpu.make_async_copy(
                tile_ref.at[sender, 0:slots],
                pool_ref.at[
                    :,
                    part * half : (part + 1) * half,
                    :,
                    head * HEAD_FEATURES : (head + 1) * HEAD_FEATURES,
                ],
                sems.at[sender],
            )
        )
        copies[-1].start()

    first = pool_rows + GROUP * local

    def back(x, places):
        return pltpu.roll(x, 128 - places, 1)

    heads = own_refs[0].shape[0]
    stacked = [
        jnp.concatenate([ref[...].reshape(heads, 2, local, 128)[:, i] for ref in own_refs[1::2]])
        for i in range(2)
    ]
    peaks = [stacked[0].reshape(-1, 128)]
    sums = [stacked[1].reshape(-1, 128)]
    for part in range(2):
        terms = came_ref[part::2, first : first + 2 * local, :].astype(jnp.float32)
        terms = terms[:, :local].reshape(-1, 128)
        terms = (terms + back(terms, GROUP)) + back(terms, 2 * GROUP)
        peaks.append(terms)
        sums.append(back(terms, 3 * GROUP))
    peak = jnp.maximum(jnp.maximum(peaks[0], peaks[1]), peaks[2])
    scales = [jnp.exp(p - peak) for p in peaks]
    total = (sums[0] * scales[0] + sums[1] * scales[1]) + sums[2] * scales[2]
    scales = [s / total for s in scales]

    for head in range(KEY_VALUE_HEADS):
        numer_ref = own_refs[head // heads * 2]
        mine_at = slice(head * local, (head + 1) * local)
        for g in range(0, GROUP, 2):
            rows = slice(g * local, (g + 2) * local)
            numers = [numer_ref[head % heads, g : g + 2].reshape(2 * local, HEAD_FEATURES)] + [
                came_ref[
                    2 * head + part, pool_rows + g * local : pool_rows + (g + 2) * local, :
                ].astype(jnp.float32)
                for part in range(2)
            ]
            for k in range(2):
                mine = [n[k * local : (k + 1) * local] for n in numers]
                by = [s[mine_at, g + k : g + k + 1] for s in scales]
                value = (mine[0] * by[0] + mine[1] * by[1]) + mine[2] * by[2]
                column = (head * GROUP + g + k) * HEAD_FEATURES
                out_ref[:, column : column + HEAD_FEATURES] = value.astype(jnp.bfloat16)

    for copy in copies:
        copy.wait()


def finish(came, own, local, slots):
    senders, rows, features = came.shape
    half = PAGE_TOKENS // 2
    tiles = came.reshape(senders, rows // (2 * half), half, 2, features)
    return pl.pallas_call(
        finish_kernel,
        out_shape=(
            jax.ShapeDtypeStruct((local, QUERY_HEADS * HEAD_FEATURES), jnp.bfloat16),
            jax.ShapeDtypeStruct(
                (slots, PAGE_TOKENS, 2, KEY_VALUE_HEADS * HEAD_FEATURES), jnp.bfloat16
            ),
        ),
        in_specs=[
            pl.BlockSpec(memory_space=pl.ANY),
        ]
        + [pl.BlockSpec(memory_space=pltpu.VMEM)] * (1 + len(own)),
        out_specs=(pl.BlockSpec(memory_space=pltpu.VMEM), pl.BlockSpec(memory_space=pl.ANY)),
        scratch_shapes=[pltpu.SemaphoreType.DMA((senders,))],
        compiler_params=pltpu.CompilerParams(vmem_limit_bytes=32 * 1024 * 1024),
        cost_estimate=pl.CostEstimate(
            flops=6 * local * QUERY_HEADS * HEAD_FEATURES,
            bytes_accessed=4 * 1024 * 1024,
            transcendentals=0,
        ),
    )(tiles, came, *own)


def choose_kernel(listed_ref, page_ref, out_ref, held_ref, reader_ref, sems, list_sem):
    fetch = pltpu.make_async_copy(listed_ref, reader_ref, list_sem)
    fetch.start()
    copies = []
    sources = page_ref.shape[0]
    for source in range(sources):
        page = page_ref[source]
        for head in range(KEY_VALUE_HEADS):
            held_ref[source, head] = page[:, :, head * HEAD_FEATURES : (head + 1) * HEAD_FEATURES]
        copies.append(
            lambda source=source: pltpu.make_async_copy(
                held_ref.at[source], out_ref.at[reader_ref[source]], sems.at[source]
            )
        )
        if source == sources * 5 // 8:
            fetch.wait()
            for copy in copies:
                copy().start()
        elif source > sources * 5 // 8:
            copies[-1]().start()
    for copy in copies:
        copy().wait()


def choose(match, pages):
    instances, tokens = pages.shape[:2]
    sources = jnp.arange(instances, dtype=match.dtype)
    reader = jnp.sum(
        jnp.where(match[None, :] == sources[:, None], sources[None, :], 0), axis=1, dtype=match.dtype
    )
    shape = (instances, KEY_VALUE_HEADS, tokens, 2, HEAD_FEATURES)
    return pl.pallas_call(
        choose_kernel,
        out_shape=jax.ShapeDtypeStruct(shape, pages.dtype),
        in_specs=[
            pl.BlockSpec(memory_space=pl.ANY),
            pl.BlockSpec(memory_space=pltpu.VMEM),
        ],
        out_specs=pl.BlockSpec(memory_space=pl.ANY),
        scratch_shapes=[
            pltpu.VMEM(shape, pages.dtype),
            pltpu.SMEM((instances,), jnp.int32),
            pltpu.SemaphoreType.DMA((instances,)),
            pltpu.SemaphoreType.DMA,
        ],
        compiler_params=pltpu.CompilerParams(vmem_limit_bytes=16 * 1024 * 1024),
        cost_estimate=pl.CostEstimate(
            flops=0, bytes_accessed=4 * 1024 * 1024, transcendentals=0
        ),
    )(reader, pages)


def exchange(held, member, n_samp, place, axis):
    bit = (member >> place) & 1
    if place:
        half = held.shape[0] // 2
        kept = lax.dynamic_slice_in_dim(held, bit * half, half, 0)
        sent = lax.dynamic_slice_in_dim(held, (1 - bit) * half, half, 0)
    else:
        kept = sent = held
    came = lax.ppermute(sent, "samp", [(i, i ^ (1 << place)) for i in range(n_samp)])
    return jnp.stack(
        [jnp.where(bit == 0, kept, came), jnp.where(bit == 0, came, kept)], axis=axis
    )


def body(n_inst, n_samp, prompt_key_values, match, page_list, queries, sample_key_values, gen_len):
    local_total = queries.shape[1]
    pages_dev = page_list.shape[2]
    half = PAGE_TOKENS // 2
    member = lax.axis_index("samp")
    local_queries = queries[0]

    pages = lax.all_to_all(prompt_key_values, "inst", split_axis=1, concat_axis=0, tiled=True)

    cache = sample_key_values[0]
    grouped = local_queries.reshape(local_total, KEY_VALUE_HEADS, GROUP, HEAD_FEATURES)
    grouped = jnp.pad(grouped, ((0, 0), (0, 0), (0, 16 - GROUP), (0, 0)))
    own = partial_own(gen_len[0], grouped, cache, 0, 2)

    held = local_queries.reshape(local_total, KEY_VALUE_HEADS, WIDTH).transpose(1, 0, 2)
    held = exchange(held, member, n_samp, 3, 1)
    held = exchange(held, member, n_samp, 2, 2)

    listed = page_list[0].reshape(-1)
    place = (listed % pages_dev) * n_samp + listed // pages_dev

    chosen = choose(match, pages).reshape(n_inst * n_samp, half * 2, HEAD_FEATURES)
    chosen, held, grouped, own = lax.optimization_barrier((chosen, held, grouped, own))
    pairs = lax.all_to_all(chosen, ("inst", "samp"), split_axis=0, concat_axis=0, tiled=True)

    own = own + partial_own(gen_len[0], grouped, cache, 1, 2)
    held = exchange(held, member, n_samp, 1, 3)
    held = exchange(held, member, n_samp, 0, 4)
    head_queries = held.reshape(n_samp * local_total, WIDTH)
    pairs, place, head_queries, own = lax.optimization_barrier((pairs, place, head_queries, own))

    sent = partial_shared(place, head_queries, pairs, n_samp)
    came = lax.all_to_all(sent, "samp", split_axis=0, concat_axis=0, tiled=True)
    attended, page_pool = finish(came, own, local_total, pages_dev)
    return (attended[None], page_pool[None])


def solution(mesh):
    in_specs = (
        P("inst", "samp", None, None),
        P(),
        P("inst", None, None),
        P("inst", "samp", None),
        P("inst", "samp", None, None, None),
        P("inst", "samp"),
    )
    out_specs = (P("inst", "samp", None), P("inst", "samp", None, None, None))
    step = functools.partial(body, mesh.shape["inst"], mesh.shape["samp"])
    return jax.shard_map(step, mesh=mesh, in_specs=in_specs, out_specs=out_specs, check_vma=False)
```

```python
import functools
import math

import jax
import jax.numpy as jnp
from jax import lax
from jax.experimental import pallas as pl
from jax.experimental.pallas import tpu as pltpu
from jax.sharding import PartitionSpec as P

QUERY_HEADS = 96
KEY_VALUE_HEADS = 8
HEAD_FEATURES = 128
PAGE_TOKENS = 16
GROUP = QUERY_HEADS // KEY_VALUE_HEADS
WIDTH = GROUP * HEAD_FEATURES
SCALE = HEAD_FEATURES ** (-0.5)


def own_kernel(head_at, length_ref, query_ref, cache_ref, numer_ref, stats_ref):
    samples, positions = cache_ref.shape[:2]
    factor = SCALE * math.log2(math.e)
    rows = query_ref.shape[2]
    column = lax.broadcasted_iota(jnp.int32, (rows, 2 * positions), 1)
    diagonal = lax.broadcasted_iota(jnp.int32, (rows, 128), 0) == lax.broadcasted_iota(
        jnp.int32, (rows, 128), 1
    )

    def across(x):
        return jnp.sum(jnp.where(diagonal, x, 0.0), axis=0, keepdims=True)

    def one_head(head, carry):
        start = pl.multiple_of(head * HEAD_FEATURES, HEAD_FEATURES)
        for sample in range(samples):
            live = (column % 2 == 0) & (column < 2 * length_ref[sample])
            both = cache_ref[sample, :, :, pl.ds(start, HEAD_FEATURES)].reshape(
                2 * positions, HEAD_FEATURES
            )
            scores = lax.dot_general(
                query_ref[sample, head_at + head], both, (((1,), (1,)), ((), ())),
                preferred_element_type=jnp.float32,
            )
            top = jnp.max(jnp.where(live, scores, -jnp.inf), axis=-1, keepdims=True)
            weights = jnp.where(live, jnp.exp2((scores - top) * factor), 0.0)
            total = jnp.sum(weights, axis=-1, keepdims=True)
            onto_values = pltpu.roll(weights, 1, 1).astype(jnp.bfloat16)
            numer = jnp.dot(onto_values, both, preferred_element_type=jnp.float32)
            numer_ref[head, :, sample, :] = numer[:GROUP]
            stats_ref[head, 0, sample : sample + 1, :] = across(top * SCALE)
            stats_ref[head, 1, sample : sample + 1, :] = across(total)
        return carry

    lax.fori_loop(0, numer_ref.shape[0], one_head, 0)


def partial_own(lengths, grouped, cache, which, parts):
    samples, positions = cache.shape[:2]
    heads = KEY_VALUE_HEADS // parts
    block = (samples, positions, 2, heads * HEAD_FEATURES)
    return pl.pallas_call(
        functools.partial(own_kernel, which * heads),
        grid=(1,),
        out_shape=(
            jax.ShapeDtypeStruct((heads, GROUP, samples, HEAD_FEATURES), jnp.float32),
            jax.ShapeDtypeStruct((heads, 2, samples, 128), jnp.float32),
        ),
        in_specs=[
            pl.BlockSpec(memory_space=pltpu.SMEM),
            pl.BlockSpec(memory_space=pltpu.VMEM),
            pl.BlockSpec(block, lambda i: (0, 0, 0, which)),
        ],
        out_specs=(
            pl.BlockSpec(memory_space=pltpu.VMEM),
            pl.BlockSpec(memory_space=pltpu.VMEM),
        ),
        compiler_params=pltpu.CompilerParams(vmem_limit_bytes=24 * 1024 * 1024),
        cost_estimate=pl.CostEstimate(flops=0, bytes_accessed=65536, transcendentals=0),
    )(lengths, grouped, cache)


def split3(x):
    high = x.astype(jnp.bfloat16)
    rest = x - high.astype(jnp.float32)
    middle = rest.astype(jnp.bfloat16)
    low = (rest - middle.astype(jnp.float32)).astype(jnp.bfloat16)
    return high, middle, low


def shared_kernel(
    listed_ref, query_ref, pair_ref, out_ref, key_ref, value_ref, wide_ref, place_ref, list_sem
):
    pieces = pair_ref.shape[0]
    samples = query_ref.shape[0]
    owners, rows = out_ref.shape[0], pair_ref.shape[1]
    slots = pieces // owners
    local = samples // owners

    fetch = pltpu.make_async_copy(listed_ref, place_ref, list_sem)
    fetch.start()
    for step in range(pieces // 16):
        wide = step % wide_ref.shape[0]
        both = pair_ref[step * 16 : (step + 1) * 16].reshape(256, HEAD_FEATURES)
        wide_ref[wide] = both.astype(jnp.float32)
        here = slice(step * 128, (step + 1) * 128)
        key_ref[here, :] = wide_ref[wide, pl.ds(0, 128, stride=2), :].astype(jnp.bfloat16)
        value_ref[here, :] = wide_ref[wide, pl.ds(1, 128, stride=2), :].astype(jnp.bfloat16)
    factor = SCALE * math.log2(math.e)
    lane = lax.broadcasted_iota(jnp.int32, (samples, 128), 1)
    peaks = jnp.zeros((samples, 128), jnp.float32)
    sums = jnp.zeros((samples, 128), jnp.float32)

    def side_by_side(low, high):
        low = low.reshape(owners, local, HEAD_FEATURES)
        high = high.reshape(owners, local, HEAD_FEATURES)
        return jnp.concatenate([low, high], axis=1).astype(jnp.bfloat16)

    def scores_of(g):
        query = jnp.concatenate(
            [
                query_ref[:, g * HEAD_FEATURES : (g + 1) * HEAD_FEATURES],
                query_ref[:, (g + 1) * HEAD_FEATURES : (g + 2) * HEAD_FEATURES],
            ],
            axis=0,
        )
        return lax.dot_general(
            query, key_ref[...], (((1,), (1,)), ((), ())), preferred_element_type=jnp.float32
        )

    later = scores_of(0)
    fetch.wait()
    for g in range(0, GROUP, 2):
        scores = later
        if g + 2 < GROUP:
            later = scores_of(g + 2)
        for n in range(g * pieces // GROUP, (g + 2) * pieces // GROUP):
            row = n % slots * rows
            out_ref[n // slots, row : row + rows, :] = pair_ref[place_ref[n]]
        top = jnp.max(scores, axis=-1, keepdims=True)
        weights = jnp.exp2((scores - top) * factor)
        total = jnp.sum(weights, axis=-1, keepdims=True)
        numer = jnp.dot(
            weights.astype(jnp.bfloat16), value_ref[...], preferred_element_type=jnp.float32
        )
        first = slots * rows + g * local
        out_ref[:, first : first + 2 * local, :] = side_by_side(numer[:samples], numer[samples:])
        top = top * SCALE
        peaks = jnp.where(lane == g, top[:samples], peaks)
        peaks = jnp.where(lane == g + 1, top[samples:], peaks)
        sums = jnp.where(lane == g, total[:samples], sums)
        sums = jnp.where(lane == g + 1, total[samples:], sums)

    stats = jnp.zeros((samples, 128), jnp.float32)
    for place, term in enumerate(split3(peaks) + split3(sums)):
        term = term.astype(jnp.float32)
        stats = stats + (pltpu.roll(term, place * GROUP, 1) if place else term)
    first = slots * rows + GROUP * local
    out_ref[:, first:, :] = side_by_side(stats, jnp.zeros_like(stats))


def partial_shared(place, query_rows, pairs, owners):
    samples = query_rows.shape[0]
    pieces, rows, features = pairs.shape
    tokens = pieces * rows // 2
    sent = pieces // owners * rows + (GROUP + 2) * (samples // owners)
    return pl.pallas_call(
        shared_kernel,
        out_shape=jax.ShapeDtypeStruct((owners, sent, features), jnp.bfloat16),
        in_specs=[
            pl.BlockSpec(memory_space=pl.ANY),
            pl.BlockSpec(memory_space=pltpu.VMEM),
            pl.BlockSpec(memory_space=pltpu.VMEM),
        ],
        out_specs=pl.BlockSpec(memory_space=pltpu.VMEM),
        scratch_shapes=[
            pltpu.VMEM((tokens, features), jnp.bfloat16),
            pltpu.VMEM((tokens, features), jnp.bfloat16),
            pltpu.VMEM((4, 256, features), jnp.float32),
            pltpu.SMEM((pieces,), jnp.int32),
            pltpu.SemaphoreType.DMA,
        ],
        compiler_params=pltpu.CompilerParams(vmem_limit_bytes=40 * 1024 * 1024),
        cost_estimate=pl.CostEstimate(
            flops=4 * samples * GROUP * tokens * features,
            bytes_accessed=4 * 1024 * 1024,
            transcendentals=samples * GROUP * tokens,
        ),
    )(place, query_rows, pairs)


def finish_kernel(tile_ref, came_ref, *refs):
    own_refs, (out_ref, pool_ref, sems) = refs[:-3], refs[-3:]
    senders = came_ref.shape[0]
    slots = pool_ref.shape[0]
    local = out_ref.shape[0]
    half = tile_ref.shape[2]
    pool_rows = slots * half * 2
    copies = []
    for sender in range(senders):
        head, part = sender // 2, sender % 2
        copies.append(
            pltpu.make_async_copy(
                tile_ref.at[sender, 0:slots],
                pool_ref.at[
                    :,
                    part * half : (part + 1) * half,
                    :,
                    head * HEAD_FEATURES : (head + 1) * HEAD_FEATURES,
                ],
                sems.at[sender],
            )
        )
        copies[-1].start()

    first = pool_rows + GROUP * local

    def back(x, places):
        return pltpu.roll(x, 128 - places, 1)

    heads = own_refs[0].shape[0]
    stacked = [
        jnp.concatenate([ref[...].reshape(heads, 2, local, 128)[:, i] for ref in own_refs[1::2]])
        for i in range(2)
    ]
    peaks = [stacked[0].reshape(-1, 128)]
    sums = [stacked[1].reshape(-1, 128)]
    for part in range(2):
        terms = came_ref[part::2, first : first + 2 * local, :].astype(jnp.float32)
        terms = terms[:, :local].reshape(-1, 128)
        terms = (terms + back(terms, GROUP)) + back(terms, 2 * GROUP)
        peaks.append(terms)
        sums.append(back(terms, 3 * GROUP))
    peak = jnp.maximum(jnp.maximum(peaks[0], peaks[1]), peaks[2])
    scales = [jnp.exp(p - peak) for p in peaks]
    total = (sums[0] * scales[0] + sums[1] * scales[1]) + sums[2] * scales[2]
    scales = [s / total for s in scales]

    for head in range(KEY_VALUE_HEADS):
        numer_ref = own_refs[head // heads * 2]
        mine_at = slice(head * local, (head + 1) * local)
        for g in range(0, GROUP, 2):
            rows = slice(g * local, (g + 2) * local)
            numers = [numer_ref[head % heads, g : g + 2].reshape(2 * local, HEAD_FEATURES)] + [
                came_ref[
                    2 * head + part, pool_rows + g * local : pool_rows + (g + 2) * local, :
                ].astype(jnp.float32)
                for part in range(2)
            ]
            for k in range(2):
                mine = [n[k * local : (k + 1) * local] for n in numers]
                by = [s[mine_at, g + k : g + k + 1] for s in scales]
                value = (mine[0] * by[0] + mine[1] * by[1]) + mine[2] * by[2]
                column = (head * GROUP + g + k) * HEAD_FEATURES
                out_ref[:, column : column + HEAD_FEATURES] = value.astype(jnp.bfloat16)

    for copy in copies:
        copy.wait()


def finish(came, own, local, slots):
    senders, rows, features = came.shape
    half = PAGE_TOKENS // 2
    tiles = came.reshape(senders, rows // (2 * half), half, 2, features)
    return pl.pallas_call(
        finish_kernel,
        out_shape=(
            jax.ShapeDtypeStruct((local, QUERY_HEADS * HEAD_FEATURES), jnp.bfloat16),
            jax.ShapeDtypeStruct(
                (slots, PAGE_TOKENS, 2, KEY_VALUE_HEADS * HEAD_FEATURES), jnp.bfloat16
            ),
        ),
        in_specs=[
            pl.BlockSpec(memory_space=pl.ANY),
        ]
        + [pl.BlockSpec(memory_space=pltpu.VMEM)] * (1 + len(own)),
        out_specs=(pl.BlockSpec(memory_space=pltpu.VMEM), pl.BlockSpec(memory_space=pl.ANY)),
        scratch_shapes=[pltpu.SemaphoreType.DMA((senders,))],
        compiler_params=pltpu.CompilerParams(vmem_limit_bytes=32 * 1024 * 1024),
        cost_estimate=pl.CostEstimate(
            flops=6 * local * QUERY_HEADS * HEAD_FEATURES,
            bytes_accessed=4 * 1024 * 1024,
            transcendentals=0,
        ),
    )(tiles, came, *own)


def choose_kernel(match_ref, page_ref, out_ref):
    for instance in range(out_ref.shape[0]):
        page = page_ref[match_ref[instance]]
        for head in range(KEY_VALUE_HEADS):
            out_ref[instance, head] = page[
                :, :, head * HEAD_FEATURES : (head + 1) * HEAD_FEATURES
            ]


def choose(match, pages):
    instances, tokens = pages.shape[:2]
    shape = (instances, KEY_VALUE_HEADS, tokens, 2, HEAD_FEATURES)
    return pl.pallas_call(
        choose_kernel,
        out_shape=pltpu.VMEM(shape, pages.dtype),
        in_specs=[
            pl.BlockSpec(memory_space=pltpu.SMEM),
            pl.BlockSpec(memory_space=pltpu.VMEM),
        ],
        out_specs=pl.BlockSpec(memory_space=pltpu.VMEM),
        compiler_params=pltpu.CompilerParams(vmem_limit_bytes=16 * 1024 * 1024),
        cost_estimate=pl.CostEstimate(
            flops=0, bytes_accessed=4 * 1024 * 1024, transcendentals=0
        ),
    )(match, pages)


def exchange(held, member, n_samp, place, axis):
    bit = (member >> place) & 1
    if place:
        half = held.shape[0] // 2
        kept = lax.dynamic_slice_in_dim(held, bit * half, half, 0)
        sent = lax.dynamic_slice_in_dim(held, (1 - bit) * half, half, 0)
    else:
        kept = sent = held
    came = lax.ppermute(sent, "samp", [(i, i ^ (1 << place)) for i in range(n_samp)])
    return jnp.stack(
        [jnp.where(bit == 0, kept, came), jnp.where(bit == 0, came, kept)], axis=axis
    )


def body(n_inst, n_samp, prompt_key_values, match, page_list, queries, sample_key_values, gen_len):
    local_total = queries.shape[1]
    pages_dev = page_list.shape[2]
    half = PAGE_TOKENS // 2
    member = lax.axis_index("samp")
    local_queries = queries[0]

    pages = lax.all_to_all(prompt_key_values, "inst", split_axis=1, concat_axis=0, tiled=True)

    cache = sample_key_values[0]
    grouped = local_queries.reshape(local_total, KEY_VALUE_HEADS, GROUP, HEAD_FEATURES)
    grouped = jnp.pad(grouped, ((0, 0), (0, 0), (0, 16 - GROUP), (0, 0)))
    own = partial_own(gen_len[0], grouped, cache, 0, 2)

    held = local_queries.reshape(local_total, KEY_VALUE_HEADS, WIDTH).transpose(1, 0, 2)
    held = exchange(held, member, n_samp, 3, 1)
    held = exchange(held, member, n_samp, 2, 2)

    listed = page_list[0].reshape(-1)
    place = (listed % pages_dev) * n_samp + listed // pages_dev

    chosen = choose(match, pages).reshape(n_inst * n_samp, half * 2, HEAD_FEATURES)
    chosen, held, grouped, own = lax.optimization_barrier((chosen, held, grouped, own))
    pairs = lax.all_to_all(chosen, ("inst", "samp"), split_axis=0, concat_axis=0, tiled=True)

    own = own + partial_own(gen_len[0], grouped, cache, 1, 2)
    held = exchange(held, member, n_samp, 1, 3)
    held = exchange(held, member, n_samp, 0, 4)
    head_queries = held.reshape(n_samp * local_total, WIDTH)
    pairs, place, head_queries, own = lax.optimization_barrier((pairs, place, head_queries, own))

    sent = partial_shared(place, head_queries, pairs, n_samp)
    came = lax.all_to_all(sent, "samp", split_axis=0, concat_axis=0, tiled=True)
    attended, page_pool = finish(came, own, local_total, pages_dev)
    return (attended[None], page_pool[None])


def solution(mesh):
    in_specs = (
        P("inst", "samp", None, None),
        P(),
        P("inst", None, None),
        P("inst", "samp", None),
        P("inst", "samp", None, None, None),
        P("inst", "samp"),
    )
    out_specs = (P("inst", "samp", None), P("inst", "samp", None, None, None))
    step = functools.partial(body, mesh.shape["inst"], mesh.shape["samp"])
    return jax.shard_map(step, mesh=mesh, in_specs=in_specs, out_specs=out_specs, check_vma=False)
```

```python
import functools
import math

import jax
import jax.numpy as jnp
from jax import lax
from jax.experimental import pallas as pl
from jax.experimental.pallas import tpu as pltpu
from jax.sharding import PartitionSpec as P

QUERY_HEADS = 96
KEY_VALUE_HEADS = 8
HEAD_FEATURES = 128
PAGE_TOKENS = 16
GROUP = QUERY_HEADS // KEY_VALUE_HEADS
WIDTH = GROUP * HEAD_FEATURES
SCALE = HEAD_FEATURES ** (-0.5)


def own_kernel(head_at, length_ref, query_ref, cache_ref, numer_ref, stats_ref):
    samples, positions = cache_ref.shape[:2]
    factor = SCALE * math.log2(math.e)
    rows = query_ref.shape[2]
    column = lax.broadcasted_iota(jnp.int32, (rows, 2 * positions), 1)
    diagonal = lax.broadcasted_iota(jnp.int32, (rows, 128), 0) == lax.broadcasted_iota(
        jnp.int32, (rows, 128), 1
    )

    def across(x):
        return jnp.sum(jnp.where(diagonal, x, 0.0), axis=0, keepdims=True)

    def one_head(head, carry):
        start = pl.multiple_of(head * HEAD_FEATURES, HEAD_FEATURES)
        for sample in range(samples):
            live = (column % 2 == 0) & (column < 2 * length_ref[sample])
            both = cache_ref[sample, :, :, pl.ds(start, HEAD_FEATURES)].reshape(
                2 * positions, HEAD_FEATURES
            )
            scores = lax.dot_general(
                query_ref[sample, head_at + head], both, (((1,), (1,)), ((), ())),
                preferred_element_type=jnp.float32,
            )
            top = jnp.max(jnp.where(live, scores, -jnp.inf), axis=-1, keepdims=True)
            weights = jnp.where(live, jnp.exp2((scores - top) * factor), 0.0)
            total = jnp.sum(weights, axis=-1, keepdims=True)
            onto_values = pltpu.roll(weights, 1, 1).astype(jnp.bfloat16)
            numer = jnp.dot(onto_values, both, preferred_element_type=jnp.float32)
            numer_ref[head, :, sample, :] = numer[:GROUP]
            stats_ref[head, 0, sample : sample + 1, :] = across(top * SCALE)
            stats_ref[head, 1, sample : sample + 1, :] = across(total)
        return carry

    lax.fori_loop(0, numer_ref.shape[0], one_head, 0)


def partial_own(lengths, grouped, cache, which, parts):
    samples, positions = cache.shape[:2]
    heads = KEY_VALUE_HEADS // parts
    block = (samples, positions, 2, heads * HEAD_FEATURES)
    return pl.pallas_call(
        functools.partial(own_kernel, which * heads),
        grid=(1,),
        out_shape=(
            jax.ShapeDtypeStruct((heads, GROUP, samples, HEAD_FEATURES), jnp.float32),
            jax.ShapeDtypeStruct((heads, 2, samples, 128), jnp.float32),
        ),
        in_specs=[
            pl.BlockSpec(memory_space=pltpu.SMEM),
            pl.BlockSpec(memory_space=pltpu.VMEM),
            pl.BlockSpec(block, lambda i: (0, 0, 0, which)),
        ],
        out_specs=(
            pl.BlockSpec(memory_space=pltpu.VMEM),
            pl.BlockSpec(memory_space=pltpu.VMEM),
        ),
        compiler_params=pltpu.CompilerParams(vmem_limit_bytes=24 * 1024 * 1024),
        cost_estimate=pl.CostEstimate(flops=0, bytes_accessed=65536, transcendentals=0),
    )(lengths, grouped, cache)


def split3(x):
    high = x.astype(jnp.bfloat16)
    rest = x - high.astype(jnp.float32)
    middle = rest.astype(jnp.bfloat16)
    low = (rest - middle.astype(jnp.float32)).astype(jnp.bfloat16)
    return high, middle, low


def shared_kernel(
    listed_ref, query_ref, pair_ref, out_ref, key_ref, value_ref, wide_ref, place_ref, list_sem
):
    pieces = pair_ref.shape[0]
    samples = query_ref.shape[0]
    owners, rows = out_ref.shape[0], pair_ref.shape[1]
    slots = pieces // owners
    local = samples // owners

    fetch = pltpu.make_async_copy(listed_ref, place_ref, list_sem)
    fetch.start()
    for step in range(pieces // 16):
        wide = step % wide_ref.shape[0]
        both = pair_ref[step * 16 : (step + 1) * 16].reshape(256, HEAD_FEATURES)
        wide_ref[wide] = both.astype(jnp.float32)
        here = slice(step * 128, (step + 1) * 128)
        key_ref[here, :] = wide_ref[wide, pl.ds(0, 128, stride=2), :].astype(jnp.bfloat16)
        value_ref[here, :] = wide_ref[wide, pl.ds(1, 128, stride=2), :].astype(jnp.bfloat16)
    factor = SCALE * math.log2(math.e)
    lane = lax.broadcasted_iota(jnp.int32, (samples, 128), 1)
    peaks = jnp.zeros((samples, 128), jnp.float32)
    sums = jnp.zeros((samples, 128), jnp.float32)

    def side_by_side(low, high):
        low = low.reshape(owners, local, HEAD_FEATURES)
        high = high.reshape(owners, local, HEAD_FEATURES)
        return jnp.concatenate([low, high], axis=1).astype(jnp.bfloat16)

    def scores_of(g):
        query = jnp.concatenate(
            [
                query_ref[:, g * HEAD_FEATURES : (g + 1) * HEAD_FEATURES],
                query_ref[:, (g + 1) * HEAD_FEATURES : (g + 2) * HEAD_FEATURES],
            ],
            axis=0,
        )
        return lax.dot_general(
            query, key_ref[...], (((1,), (1,)), ((), ())), preferred_element_type=jnp.float32
        )

    later = scores_of(0)
    fetch.wait()
    for g in range(0, GROUP, 2):
        scores = later
        if g + 2 < GROUP:
            later = scores_of(g + 2)
        for n in range(g * pieces // GROUP, (g + 2) * pieces // GROUP):
            row = n % slots * rows
            out_ref[n // slots, row : row + rows, :] = pair_ref[place_ref[n]]
        top = jnp.max(scores, axis=-1, keepdims=True)
        weights = jnp.exp2((scores - top) * factor)
        total = jnp.sum(weights, axis=-1, keepdims=True)
        numer = jnp.dot(
            weights.astype(jnp.bfloat16), value_ref[...], preferred_element_type=jnp.float32
        )
        first = slots * rows + g * local
        out_ref[:, first : first + 2 * local, :] = side_by_side(numer[:samples], numer[samples:])
        top = top * SCALE
        peaks = jnp.where(lane == g, top[:samples], peaks)
        peaks = jnp.where(lane == g + 1, top[samples:], peaks)
        sums = jnp.where(lane == g, total[:samples], sums)
        sums = jnp.where(lane == g + 1, total[samples:], sums)

    stats = jnp.zeros((samples, 128), jnp.float32)
    for place, term in enumerate(split3(peaks) + split3(sums)):
        term = term.astype(jnp.float32)
        stats = stats + (pltpu.roll(term, place * GROUP, 1) if place else term)
    first = slots * rows + GROUP * local
    out_ref[:, first:, :] = side_by_side(stats, jnp.zeros_like(stats))


def partial_shared(place, query_rows, pairs, owners):
    samples = query_rows.shape[0]
    pieces, rows, features = pairs.shape
    tokens = pieces * rows // 2
    sent = pieces // owners * rows + (GROUP + 2) * (samples // owners)
    return pl.pallas_call(
        shared_kernel,
        out_shape=jax.ShapeDtypeStruct((owners, sent, features), jnp.bfloat16),
        in_specs=[
            pl.BlockSpec(memory_space=pl.ANY),
            pl.BlockSpec(memory_space=pltpu.VMEM),
            pl.BlockSpec(memory_space=pltpu.VMEM),
        ],
        out_specs=pl.BlockSpec(memory_space=pltpu.VMEM),
        scratch_shapes=[
            pltpu.VMEM((tokens, features), jnp.bfloat16),
            pltpu.VMEM((tokens, features), jnp.bfloat16),
            pltpu.VMEM((4, 256, features), jnp.float32),
            pltpu.SMEM((pieces,), jnp.int32),
            pltpu.SemaphoreType.DMA,
        ],
        compiler_params=pltpu.CompilerParams(vmem_limit_bytes=40 * 1024 * 1024),
        cost_estimate=pl.CostEstimate(
            flops=4 * samples * GROUP * tokens * features,
            bytes_accessed=4 * 1024 * 1024,
            transcendentals=samples * GROUP * tokens,
        ),
    )(place, query_rows, pairs)


def finish_kernel(tile_ref, came_ref, *refs):
    own_refs, (to_ref, pool_ref, out_ref, sems) = refs[:-4], refs[-4:]
    senders = came_ref.shape[0]
    slots = pool_ref.shape[0]
    local = out_ref.shape[0]
    half = tile_ref.shape[2]
    pool_rows = slots * half * 2
    copies = []
    for sender in range(senders):
        head, part = sender // 2, sender % 2
        copies.append(
            pltpu.make_async_copy(
                tile_ref.at[sender, 0:slots],
                pool_ref.at[
                    :,
                    part * half : (part + 1) * half,
                    :,
                    head * HEAD_FEATURES : (head + 1) * HEAD_FEATURES,
                ],
                sems.at[sender],
            )
        )
        copies[-1].start()

    first = pool_rows + GROUP * local

    def back(x, places):
        return pltpu.roll(x, 128 - places, 1)

    heads = own_refs[0].shape[0]
    stacked = [
        jnp.concatenate([ref[...].reshape(heads, 2, local, 128)[:, i] for ref in own_refs[1::2]])
        for i in range(2)
    ]
    peaks = [stacked[0].reshape(-1, 128)]
    sums = [stacked[1].reshape(-1, 128)]
    for part in range(2):
        terms = came_ref[part::2, first : first + 2 * local, :].astype(jnp.float32)
        terms = terms[:, :local].reshape(-1, 128)
        terms = (terms + back(terms, GROUP)) + back(terms, 2 * GROUP)
        peaks.append(terms)
        sums.append(back(terms, 3 * GROUP))
    peak = jnp.maximum(jnp.maximum(peaks[0], peaks[1]), peaks[2])
    scales = [jnp.exp(p - peak) for p in peaks]
    total = (sums[0] * scales[0] + sums[1] * scales[1]) + sums[2] * scales[2]
    scales = [s / total for s in scales]

    for head in range(KEY_VALUE_HEADS):
        numer_ref = own_refs[head // heads * 2]
        mine_at = slice(head * local, (head + 1) * local)
        for g in range(0, GROUP, 2):
            rows = slice(g * local, (g + 2) * local)
            numers = [numer_ref[head % heads, g : g + 2].reshape(2 * local, HEAD_FEATURES)] + [
                came_ref[
                    2 * head + part, pool_rows + g * local : pool_rows + (g + 2) * local, :
                ].astype(jnp.float32)
                for part in range(2)
            ]
            for k in range(2):
                mine = [n[k * local : (k + 1) * local] for n in numers]
                by = [s[mine_at, g + k : g + k + 1] for s in scales]
                value = (mine[0] * by[0] + mine[1] * by[1]) + mine[2] * by[2]
                column = (head * GROUP + g + k) * HEAD_FEATURES
                out_ref[:, column : column + HEAD_FEATURES] = value.astype(jnp.bfloat16)
        if head % 4 == 3:
            columns = slice((head - 3) * WIDTH, (head + 1) * WIDTH)
            copies.append(
                pltpu.make_async_copy(
                    out_ref.at[:, columns], to_ref.at[:, columns], sems.at[senders + head]
                )
            )
            copies[-1].start()

    for copy in copies:
        copy.wait()


def finish(came, own, local, slots):
    senders, rows, features = came.shape
    half = PAGE_TOKENS // 2
    tiles = came.reshape(senders, rows // (2 * half), half, 2, features)
    return pl.pallas_call(
        finish_kernel,
        out_shape=(
            jax.ShapeDtypeStruct((local, QUERY_HEADS * HEAD_FEATURES), jnp.bfloat16),
            jax.ShapeDtypeStruct(
                (slots, PAGE_TOKENS, 2, KEY_VALUE_HEADS * HEAD_FEATURES), jnp.bfloat16
            ),
        ),
        in_specs=[
            pl.BlockSpec(memory_space=pl.ANY),
        ]
        + [pl.BlockSpec(memory_space=pltpu.VMEM)] * (1 + len(own)),
        out_specs=(pl.BlockSpec(memory_space=pl.ANY), pl.BlockSpec(memory_space=pl.ANY)),
        scratch_shapes=[
            pltpu.VMEM((local, QUERY_HEADS * HEAD_FEATURES), jnp.bfloat16),
            pltpu.SemaphoreType.DMA((senders + KEY_VALUE_HEADS,)),
        ],
        compiler_params=pltpu.CompilerParams(vmem_limit_bytes=32 * 1024 * 1024),
        cost_estimate=pl.CostEstimate(
            flops=6 * local * QUERY_HEADS * HEAD_FEATURES,
            bytes_accessed=4 * 1024 * 1024,
            transcendentals=0,
        ),
    )(tiles, came, *own)


def choose_kernel(listed_ref, page_ref, out_ref, held_ref, reader_ref, sems, list_sem):
    fetch = pltpu.make_async_copy(listed_ref, reader_ref, list_sem)
    fetch.start()
    copies = []
    sources = page_ref.shape[0]
    for source in range(sources):
        page = page_ref[source]
        for head in range(KEY_VALUE_HEADS):
            held_ref[source, head] = page[:, :, head * HEAD_FEATURES : (head + 1) * HEAD_FEATURES]
        copies.append(
            lambda source=source: pltpu.make_async_copy(
                held_ref.at[source], out_ref.at[reader_ref[source]], sems.at[source]
            )
        )
        if source == sources * 5 // 8:
            fetch.wait()
            for copy in copies:
                copy().start()
        elif source > sources * 5 // 8:
            copies[-1]().start()
    for copy in copies:
        copy().wait()


def choose(match, pages):
    instances, tokens = pages.shape[:2]
    sources = jnp.arange(instances, dtype=match.dtype)
    reader = jnp.sum(
        jnp.where(match[None, :] == sources[:, None], sources[None, :], 0), axis=1, dtype=match.dtype
    )
    shape = (instances, KEY_VALUE_HEADS, tokens, 2, HEAD_FEATURES)
    return pl.pallas_call(
        choose_kernel,
        out_shape=jax.ShapeDtypeStruct(shape, pages.dtype),
        in_specs=[
            pl.BlockSpec(memory_space=pl.ANY),
            pl.BlockSpec(memory_space=pltpu.VMEM),
        ],
        out_specs=pl.BlockSpec(memory_space=pl.ANY),
        scratch_shapes=[
            pltpu.VMEM(shape, pages.dtype),
            pltpu.SMEM((instances,), jnp.int32),
            pltpu.SemaphoreType.DMA((instances,)),
            pltpu.SemaphoreType.DMA,
        ],
        compiler_params=pltpu.CompilerParams(vmem_limit_bytes=16 * 1024 * 1024),
        cost_estimate=pl.CostEstimate(
            flops=0, bytes_accessed=4 * 1024 * 1024, transcendentals=0
        ),
    )(reader, pages)


def exchange(held, member, n_samp, place, axis):
    bit = (member >> place) & 1
    if place:
        half = held.shape[0] // 2
        kept = lax.dynamic_slice_in_dim(held, bit * half, half, 0)
        sent = lax.dynamic_slice_in_dim(held, (1 - bit) * half, half, 0)
    else:
        kept = sent = held
    came = lax.ppermute(sent, "samp", [(i, i ^ (1 << place)) for i in range(n_samp)])
    return jnp.stack(
        [jnp.where(bit == 0, kept, came), jnp.where(bit == 0, came, kept)], axis=axis
    )


def body(n_inst, n_samp, prompt_key_values, match, page_list, queries, sample_key_values, gen_len):
    local_total = queries.shape[1]
    pages_dev = page_list.shape[2]
    half = PAGE_TOKENS // 2
    member = lax.axis_index("samp")
    local_queries = queries[0]

    pages = lax.all_to_all(prompt_key_values, "inst", split_axis=1, concat_axis=0, tiled=True)

    cache = sample_key_values[0]
    grouped = local_queries.reshape(local_total, KEY_VALUE_HEADS, GROUP, HEAD_FEATURES)
    grouped = jnp.pad(grouped, ((0, 0), (0, 0), (0, 16 - GROUP), (0, 0)))
    own = partial_own(gen_len[0], grouped, cache, 0, 2)

    held = local_queries.reshape(local_total, KEY_VALUE_HEADS, WIDTH).transpose(1, 0, 2)
    held = exchange(held, member, n_samp, 3, 1)
    held = exchange(held, member, n_samp, 2, 2)

    listed = page_list[0].reshape(-1)
    place = (listed % pages_dev) * n_samp + listed // pages_dev

    chosen = choose(match, pages).reshape(n_inst * n_samp, half * 2, HEAD_FEATURES)
    chosen, held, grouped, own = lax.optimization_barrier((chosen, held, grouped, own))
    pairs = lax.all_to_all(chosen, ("inst", "samp"), split_axis=0, concat_axis=0, tiled=True)

    own = own + partial_own(gen_len[0], grouped, cache, 1, 2)
    held = exchange(held, member, n_samp, 1, 3)
    held = exchange(held, member, n_samp, 0, 4)
    head_queries = held.reshape(n_samp * local_total, WIDTH)
    pairs, place, head_queries, own = lax.optimization_barrier((pairs, place, head_queries, own))

    sent = partial_shared(place, head_queries, pairs, n_samp)
    came = lax.all_to_all(sent, "samp", split_axis=0, concat_axis=0, tiled=True)
    attended, page_pool = finish(came, own, local_total, pages_dev)
    return (attended[None], page_pool[None])


def solution(mesh):
    in_specs = (
        P("inst", "samp", None, None),
        P(),
        P("inst", None, None),
        P("inst", "samp", None),
        P("inst", "samp", None, None, None),
        P("inst", "samp"),
    )
    out_specs = (P("inst", "samp", None), P("inst", "samp", None, None, None))
    step = functools.partial(body, mesh.shape["inst"], mesh.shape["samp"])
    return jax.shard_map(step, mesh=mesh, in_specs=in_specs, out_specs=out_specs, check_vma=False)
```

```python
import functools
import math

import jax
import jax.numpy as jnp
from jax import lax
from jax.experimental import pallas as pl
from jax.experimental.pallas import tpu as pltpu
from jax.sharding import PartitionSpec as P

QUERY_HEADS = 96
KEY_VALUE_HEADS = 8
HEAD_FEATURES = 128
PAGE_TOKENS = 16
GROUP = QUERY_HEADS // KEY_VALUE_HEADS
WIDTH = GROUP * HEAD_FEATURES
SCALE = HEAD_FEATURES ** (-0.5)


def own_kernel(head_at, length_ref, query_ref, cache_ref, numer_ref, stats_ref):
    samples, positions = cache_ref.shape[:2]
    factor = SCALE * math.log2(math.e)
    rows = query_ref.shape[2]
    column = lax.broadcasted_iota(jnp.int32, (rows, 2 * positions), 1)
    diagonal = lax.broadcasted_iota(jnp.int32, (rows, 128), 0) == lax.broadcasted_iota(
        jnp.int32, (rows, 128), 1
    )

    def across(x):
        return jnp.sum(jnp.where(diagonal, x, 0.0), axis=0, keepdims=True)

    def one_head(head, carry):
        start = pl.multiple_of(head * HEAD_FEATURES, HEAD_FEATURES)
        for sample in range(samples):
            live = (column % 2 == 0) & (column < 2 * length_ref[sample])
            both = cache_ref[sample, :, :, pl.ds(start, HEAD_FEATURES)].reshape(
                2 * positions, HEAD_FEATURES
            )
            scores = lax.dot_general(
                query_ref[sample, head_at + head], both, (((1,), (1,)), ((), ())),
                preferred_element_type=jnp.float32,
            )
            top = jnp.max(jnp.where(live, scores, -jnp.inf), axis=-1, keepdims=True)
            weights = jnp.where(live, jnp.exp2((scores - top) * factor), 0.0)
            total = jnp.sum(weights, axis=-1, keepdims=True)
            onto_values = pltpu.roll(weights, 1, 1).astype(jnp.bfloat16)
            numer = jnp.dot(onto_values, both, preferred_element_type=jnp.float32)
            numer_ref[head, :, sample, :] = numer[:GROUP]
            stats_ref[head, 0, sample : sample + 1, :] = across(top * SCALE)
            stats_ref[head, 1, sample : sample + 1, :] = across(total)
        return carry

    lax.fori_loop(0, numer_ref.shape[0], one_head, 0)


def partial_own(lengths, grouped, cache, which, parts):
    samples, positions = cache.shape[:2]
    heads = KEY_VALUE_HEADS // parts
    block = (samples, positions, 2, heads * HEAD_FEATURES)
    return pl.pallas_call(
        functools.partial(own_kernel, which * heads),
        grid=(1,),
        out_shape=(
            jax.ShapeDtypeStruct((heads, GROUP, samples, HEAD_FEATURES), jnp.float32),
            jax.ShapeDtypeStruct((heads, 2, samples, 128), jnp.float32),
        ),
        in_specs=[
            pl.BlockSpec(memory_space=pltpu.SMEM),
            pl.BlockSpec(memory_space=pltpu.VMEM),
            pl.BlockSpec(block, lambda i: (0, 0, 0, which)),
        ],
        out_specs=(
            pl.BlockSpec(memory_space=pltpu.VMEM),
            pl.BlockSpec(memory_space=pltpu.VMEM),
        ),
        compiler_params=pltpu.CompilerParams(vmem_limit_bytes=24 * 1024 * 1024),
        cost_estimate=pl.CostEstimate(flops=0, bytes_accessed=65536, transcendentals=0),
    )(lengths, grouped, cache)


def split3(x):
    high = x.astype(jnp.bfloat16)
    rest = x - high.astype(jnp.float32)
    middle = rest.astype(jnp.bfloat16)
    low = (rest - middle.astype(jnp.float32)).astype(jnp.bfloat16)
    return high, middle, low


def shared_kernel(
    listed_ref, query_ref, pair_ref, out_ref, key_ref, value_ref, wide_ref, place_ref, list_sem
):
    pieces = pair_ref.shape[0]
    samples = query_ref.shape[0]
    owners, rows = out_ref.shape[0], pair_ref.shape[1]
    slots = pieces // owners
    local = samples // owners

    fetch = pltpu.make_async_copy(listed_ref, place_ref, list_sem)
    fetch.start()
    for step in range(pieces // 16):
        wide = step % wide_ref.shape[0]
        both = pair_ref[step * 16 : (step + 1) * 16].reshape(256, HEAD_FEATURES)
        wide_ref[wide] = both.astype(jnp.float32)
        here = slice(step * 128, (step + 1) * 128)
        key_ref[here, :] = wide_ref[wide, pl.ds(0, 128, stride=2), :].astype(jnp.bfloat16)
        value_ref[here, :] = wide_ref[wide, pl.ds(1, 128, stride=2), :].astype(jnp.bfloat16)
    factor = SCALE * math.log2(math.e)
    lane = lax.broadcasted_iota(jnp.int32, (samples, 128), 1)
    peaks = jnp.zeros((samples, 128), jnp.float32)
    sums = jnp.zeros((samples, 128), jnp.float32)

    def side_by_side(low, high):
        low = low.reshape(owners, local, HEAD_FEATURES)
        high = high.reshape(owners, local, HEAD_FEATURES)
        return jnp.concatenate([low, high], axis=1).astype(jnp.bfloat16)

    def scores_of(g):
        query = jnp.concatenate(
            [
                query_ref[:, g * HEAD_FEATURES : (g + 1) * HEAD_FEATURES],
                query_ref[:, (g + 1) * HEAD_FEATURES : (g + 2) * HEAD_FEATURES],
            ],
            axis=0,
        )
        return lax.dot_general(
            query, key_ref[...], (((1,), (1,)), ((), ())), preferred_element_type=jnp.float32
        )

    def send(g, weights):
        numer = jnp.dot(weights, value_ref[...], preferred_element_type=jnp.float32)
        first = slots * rows + g * local
        out_ref[:, first : first + 2 * local, :] = side_by_side(numer[:samples], numer[samples:])

    later = scores_of(0)
    fetch.wait()
    for g in range(0, GROUP, 2):
        scores = later
        if g + 2 < GROUP:
            later = scores_of(g + 2)
        for n in range(g * pieces // GROUP, (g + 2) * pieces // GROUP):
            row = n % slots * rows
            out_ref[n // slots, row : row + rows, :] = pair_ref[place_ref[n]]
        top = jnp.max(scores, axis=-1, keepdims=True)
        weights = jnp.exp2((scores - top) * factor)
        total = jnp.sum(weights, axis=-1, keepdims=True)
        weights = weights.astype(jnp.bfloat16)
        if g + 2 < GROUP:
            send(g, weights)
        top = top * SCALE
        peaks = jnp.where(lane == g, top[:samples], peaks)
        peaks = jnp.where(lane == g + 1, top[samples:], peaks)
        sums = jnp.where(lane == g, total[:samples], sums)
        sums = jnp.where(lane == g + 1, total[samples:], sums)

    stats = jnp.zeros((samples, 128), jnp.float32)
    for place, term in enumerate(split3(peaks) + split3(sums)):
        term = term.astype(jnp.float32)
        stats = stats + (pltpu.roll(term, place * GROUP, 1) if place else term)
    first = slots * rows + GROUP * local
    out_ref[:, first:, :] = side_by_side(stats, jnp.zeros_like(stats))
    send(GROUP - 2, weights)


def partial_shared(place, query_rows, pairs, owners):
    samples = query_rows.shape[0]
    pieces, rows, features = pairs.shape
    tokens = pieces * rows // 2
    sent = pieces // owners * rows + (GROUP + 2) * (samples // owners)
    return pl.pallas_call(
        shared_kernel,
        out_shape=jax.ShapeDtypeStruct((owners, sent, features), jnp.bfloat16),
        in_specs=[
            pl.BlockSpec(memory_space=pl.ANY),
            pl.BlockSpec(memory_space=pltpu.VMEM),
            pl.BlockSpec(memory_space=pltpu.VMEM),
        ],
        out_specs=pl.BlockSpec(memory_space=pltpu.VMEM),
        scratch_shapes=[
            pltpu.VMEM((tokens, features), jnp.bfloat16),
            pltpu.VMEM((tokens, features), jnp.bfloat16),
            pltpu.VMEM((4, 256, features), jnp.float32),
            pltpu.SMEM((pieces,), jnp.int32),
            pltpu.SemaphoreType.DMA,
        ],
        compiler_params=pltpu.CompilerParams(vmem_limit_bytes=40 * 1024 * 1024),
        cost_estimate=pl.CostEstimate(
            flops=4 * samples * GROUP * tokens * features,
            bytes_accessed=4 * 1024 * 1024,
            transcendentals=samples * GROUP * tokens,
        ),
    )(place, query_rows, pairs)


def finish_kernel(tile_ref, came_ref, *refs):
    own_refs, (to_ref, pool_ref, out_ref, sems) = refs[:-4], refs[-4:]
    senders = came_ref.shape[0]
    slots = pool_ref.shape[0]
    local = out_ref.shape[0]
    half = tile_ref.shape[2]
    pool_rows = slots * half * 2
    copies = []
    for sender in range(senders):
        head, part = sender // 2, sender % 2
        copies.append(
            pltpu.make_async_copy(
                tile_ref.at[sender, 0:slots],
                pool_ref.at[
                    :,
                    part * half : (part + 1) * half,
                    :,
                    head * HEAD_FEATURES : (head + 1) * HEAD_FEATURES,
                ],
                sems.at[sender],
            )
        )
        copies[-1].start()

    first = pool_rows + GROUP * local

    def back(x, places):
        return pltpu.roll(x, 128 - places, 1)

    heads = own_refs[0].shape[0]
    stacked = [
        jnp.concatenate([ref[...].reshape(heads, 2, local, 128)[:, i] for ref in own_refs[1::2]])
        for i in range(2)
    ]
    peaks = [stacked[0].reshape(-1, 128)]
    sums = [stacked[1].reshape(-1, 128)]
    for part in range(2):
        terms = came_ref[part::2, first : first + 2 * local, :].astype(jnp.float32)
        terms = terms[:, :local].reshape(-1, 128)
        terms = (terms + back(terms, GROUP)) + back(terms, 2 * GROUP)
        peaks.append(terms)
        sums.append(back(terms, 3 * GROUP))
    peak = jnp.maximum(jnp.maximum(peaks[0], peaks[1]), peaks[2])
    scales = [jnp.exp(p - peak) for p in peaks]
    total = (sums[0] * scales[0] + sums[1] * scales[1]) + sums[2] * scales[2]
    scales = [s / total for s in scales]

    for head in range(KEY_VALUE_HEADS):
        numer_ref = own_refs[head // heads * 2]
        mine_at = slice(head * local, (head + 1) * local)
        for g in range(0, GROUP, 2):
            rows = slice(g * local, (g + 2) * local)
            numers = [numer_ref[head % heads, g : g + 2].reshape(2 * local, HEAD_FEATURES)] + [
                came_ref[
                    2 * head + part, pool_rows + g * local : pool_rows + (g + 2) * local, :
                ].astype(jnp.float32)
                for part in range(2)
            ]
            for k in range(2):
                mine = [n[k * local : (k + 1) * local] for n in numers]
                by = [s[mine_at, g + k : g + k + 1] for s in scales]
                value = (mine[0] * by[0] + mine[1] * by[1]) + mine[2] * by[2]
                column = (head * GROUP + g + k) * HEAD_FEATURES
                out_ref[:, column : column + HEAD_FEATURES] = value.astype(jnp.bfloat16)
        columns = slice(head * WIDTH, (head + 1) * WIDTH)
        copies.append(
            pltpu.make_async_copy(
                out_ref.at[:, columns], to_ref.at[:, columns], sems.at[senders + head]
            )
        )
        copies[-1].start()

    for copy in copies:
        copy.wait()


def finish(came, own, local, slots):
    senders, rows, features = came.shape
    half = PAGE_TOKENS // 2
    tiles = came.reshape(senders, rows // (2 * half), half, 2, features)
    return pl.pallas_call(
        finish_kernel,
        out_shape=(
            jax.ShapeDtypeStruct((local, QUERY_HEADS * HEAD_FEATURES), jnp.bfloat16),
            jax.ShapeDtypeStruct(
                (slots, PAGE_TOKENS, 2, KEY_VALUE_HEADS * HEAD_FEATURES), jnp.bfloat16
            ),
        ),
        in_specs=[
            pl.BlockSpec(memory_space=pl.ANY),
        ]
        + [pl.BlockSpec(memory_space=pltpu.VMEM)] * (1 + len(own)),
        out_specs=(pl.BlockSpec(memory_space=pl.ANY), pl.BlockSpec(memory_space=pl.ANY)),
        scratch_shapes=[
            pltpu.VMEM((local, QUERY_HEADS * HEAD_FEATURES), jnp.bfloat16),
            pltpu.SemaphoreType.DMA((senders + KEY_VALUE_HEADS,)),
        ],
        compiler_params=pltpu.CompilerParams(vmem_limit_bytes=32 * 1024 * 1024),
        cost_estimate=pl.CostEstimate(
            flops=6 * local * QUERY_HEADS * HEAD_FEATURES,
            bytes_accessed=4 * 1024 * 1024,
            transcendentals=0,
        ),
    )(tiles, came, *own)


def choose_kernel(listed_ref, page_ref, out_ref, held_ref, reader_ref, sems, list_sem):
    fetch = pltpu.make_async_copy(listed_ref, reader_ref, list_sem)
    fetch.start()
    copies = []
    sources = page_ref.shape[0]
    for source in range(sources):
        page = page_ref[source]
        for head in range(KEY_VALUE_HEADS):
            held_ref[source, head] = page[:, :, head * HEAD_FEATURES : (head + 1) * HEAD_FEATURES]
        copies.append(
            lambda source=source: pltpu.make_async_copy(
                held_ref.at[source], out_ref.at[reader_ref[source]], sems.at[source]
            )
        )
        if source == sources * 5 // 8:
            fetch.wait()
            for copy in copies:
                copy().start()
        elif source > sources * 5 // 8:
            copies[-1]().start()
    for copy in copies:
        copy().wait()


def choose(match, pages):
    instances, tokens = pages.shape[:2]
    sources = jnp.arange(instances, dtype=match.dtype)
    reader = jnp.sum(
        jnp.where(match[None, :] == sources[:, None], sources[None, :], 0), axis=1, dtype=match.dtype
    )
    shape = (instances, KEY_VALUE_HEADS, tokens, 2, HEAD_FEATURES)
    return pl.pallas_call(
        choose_kernel,
        out_shape=jax.ShapeDtypeStruct(shape, pages.dtype),
        in_specs=[
            pl.BlockSpec(memory_space=pl.ANY),
            pl.BlockSpec(memory_space=pltpu.VMEM),
        ],
        out_specs=pl.BlockSpec(memory_space=pl.ANY),
        scratch_shapes=[
            pltpu.VMEM(shape, pages.dtype),
            pltpu.SMEM((instances,), jnp.int32),
            pltpu.SemaphoreType.DMA((instances,)),
            pltpu.SemaphoreType.DMA,
        ],
        compiler_params=pltpu.CompilerParams(vmem_limit_bytes=16 * 1024 * 1024),
        cost_estimate=pl.CostEstimate(
            flops=0, bytes_accessed=4 * 1024 * 1024, transcendentals=0
        ),
    )(reader, pages)


def exchange(held, member, n_samp, place, axis):
    bit = (member >> place) & 1
    if place:
        half = held.shape[0] // 2
        kept = lax.dynamic_slice_in_dim(held, bit * half, half, 0)
        sent = lax.dynamic_slice_in_dim(held, (1 - bit) * half, half, 0)
    else:
        kept = sent = held
    came = lax.ppermute(sent, "samp", [(i, i ^ (1 << place)) for i in range(n_samp)])
    return jnp.stack(
        [jnp.where(bit == 0, kept, came), jnp.where(bit == 0, came, kept)], axis=axis
    )


def body(n_inst, n_samp, prompt_key_values, match, page_list, queries, sample_key_values, gen_len):
    local_total = queries.shape[1]
    pages_dev = page_list.shape[2]
    half = PAGE_TOKENS // 2
    member = lax.axis_index("samp")
    local_queries = queries[0]

    pages = lax.all_to_all(prompt_key_values, "inst", split_axis=1, concat_axis=0, tiled=True)

    cache = sample_key_values[0]
    grouped = local_queries.reshape(local_total, KEY_VALUE_HEADS, GROUP, HEAD_FEATURES)
    grouped = jnp.pad(grouped, ((0, 0), (0, 0), (0, 16 - GROUP), (0, 0)))
    own = partial_own(gen_len[0], grouped, cache, 0, 2)

    held = local_queries.reshape(local_total, KEY_VALUE_HEADS, WIDTH).transpose(1, 0, 2)
    held = exchange(held, member, n_samp, 3, 1)
    held = exchange(held, member, n_samp, 2, 2)

    listed = page_list[0].reshape(-1)
    place = (listed % pages_dev) * n_samp + listed // pages_dev

    chosen = choose(match, pages).reshape(n_inst * n_samp, half * 2, HEAD_FEATURES)
    chosen, held, grouped, own = lax.optimization_barrier((chosen, held, grouped, own))
    pairs = lax.all_to_all(chosen, ("inst", "samp"), split_axis=0, concat_axis=0, tiled=True)

    own = own + partial_own(gen_len[0], grouped, cache, 1, 2)
    held = exchange(held, member, n_samp, 1, 3)
    held = exchange(held, member, n_samp, 0, 4)
    head_queries = held.reshape(n_samp * local_total, WIDTH)
    pairs, place, head_queries, own = lax.optimization_barrier((pairs, place, head_queries, own))

    sent = partial_shared(place, head_queries, pairs, n_samp)
    came = lax.all_to_all(sent, "samp", split_axis=0, concat_axis=0, tiled=True)
    attended, page_pool = finish(came, own, local_total, pages_dev)
    return (attended[None], page_pool[None])


def solution(mesh):
    in_specs = (
        P("inst", "samp", None, None),
        P(),
        P("inst", None, None),
        P("inst", "samp", None),
        P("inst", "samp", None, None, None),
        P("inst", "samp"),
    )
    out_specs = (P("inst", "samp", None), P("inst", "samp", None, None, None))
    step = functools.partial(body, mesh.shape["inst"], mesh.shape["samp"])
    return jax.shard_map(step, mesh=mesh, in_specs=in_specs, out_specs=out_specs, check_vma=False)
```
